32 devices in a mesh: lon: 8 (over z, y), lat: 4 (over x, core).
Axes of the slice: x: 2, y: 2, z: 4, core: 2. Of those that a mesh axis runs over, the one named last changes fastest.
Arguments:
- heat_content: float32 [1024, 2048], P('lat', 'lon'), may hold values from -6 to 6
- saltiness_anomaly: float32 [1024, 2048], P('lat', 'lon'), may hold values from -6 to 6
- water_indicator: int32 [1024, 2048], P('lat', 'lon'), may hold values 0 or 1
- gradient_kind_index: int32 [1024, 2048], P('lat', 'lon'), may hold values from 0 to 15
- gradient_kind_table: float32 [16, 2], replicated, may hold values from -1 to 1
- easterly_transit_number: float32 [1024, 2048], P('lat', 'lon'), may hold values from -0.5 to 0.5
- poleward_transit_number: float32 [1024, 2048], P('lat', 'lon'), may hold values from -0.5 to 0.5
Outputs:
- new_temperature: float32 [1024, 2048], P('lat', 'lon')
- new_salinity: float32 [1024, 2048], P('lat', 'lon')
The draws below stay inside these ranges and needn't reach their ends.
All inputs are finite; a program needn't handle non-finite values. No bound on the sum of `water_indicator` on one device may be relied on, other than what follows from the above.
Results may differ from the reference program's by a relative error of at most 0.0003.
Values sent between devices are 32-bit elements; how exact they have to be, the bound alone decides.
A program may use at most 64 MiB of HBM per device.

```python
import jax
import jax.numpy as jnp

NCLASS = 16
STEPS = 4
PARALLEL_COUNT = 1024
MERIDIAN_COUNT = 2048


def place_ends(values, own_key, least, largest):
    place = [jax.random.randint(jax.random.fold_in(own_key, axis), (), 0, length) for axis, length in enumerate(values.shape)]
    main_axis = values.shape.index(max(values.shape))
    beside = place[:main_axis] + [(place[main_axis] + 1) % values.shape[main_axis]] + place[main_axis + 1:]
    return values.at[tuple(place)].set(least).at[tuple(beside)].set(largest)


def block_levels(stream_key, extent, split, least, high):
    def one(position, parts):
        heights = jax.random.uniform(jax.random.fold_in(jax.random.fold_in(stream_key, 6), position), (parts,), jnp.float32, least / len(split), high / len(split))
        return jnp.repeat(jnp.exp(heights), extent[position] // parts).reshape((-1,) + (1,) * (len(extent) - position - 1))

    level = one(*split[0])
    for cut in split[1:]:
        level = level * one(*cut)
    return level


def gaussian(stream_key, extent, width, most, cuts=(), kind=jnp.bfloat16):
    factor_of = block_levels(stream_key, extent, cuts, -0.22, 0.18) if cuts else 1.0
    drawn = jax.random.normal(stream_key, extent, jnp.float32) * width * factor_of
    return jnp.minimum(jnp.maximum(drawn, -most), most).astype(kind)


def setup_inputs(seed: int = 0) -> dict:
    key_list = jax.random.split(jax.random.key(seed), 8)
    heat_content = gaussian(key_list[0], (PARALLEL_COUNT, MERIDIAN_COUNT), 1.0, 6.0, ((0, 4), (1, 8)), jnp.float32)
    saltiness_anomaly = gaussian(key_list[1], (PARALLEL_COUNT, MERIDIAN_COUNT), 1.0, 6.0, ((0, 4), (1, 8)), jnp.float32)
    water_indicator = place_ends((jax.random.randint(key_list[2], (PARALLEL_COUNT, MERIDIAN_COUNT), 0, 4) < 3).astype(jnp.int32), jax.random.fold_in(key_list[2], 1), 0, 1)
    gradient_kind_index = place_ends(jax.random.randint(key_list[3], (PARALLEL_COUNT, MERIDIAN_COUNT), 0, NCLASS), jax.random.fold_in(key_list[3], 1), 0, NCLASS - 1).astype(jnp.int32)
    gradient_kind_table = jnp.clip(jax.random.uniform(key_list[4], (NCLASS, 2), jnp.float32, -1.0, 1.0), -1.0, 1.0)
    easterly_transit_number = jnp.clip(jax.random.uniform(key_list[5], (PARALLEL_COUNT, MERIDIAN_COUNT), jnp.float32, -0.5, 0.5) * block_levels(key_list[5], (PARALLEL_COUNT, MERIDIAN_COUNT), ((0, 4), (1, 8)), -0.4, 0.0), -0.5, 0.5)
    poleward_transit_number = jnp.clip(jax.random.uniform(key_list[6], (PARALLEL_COUNT, MERIDIAN_COUNT), jnp.float32, -0.5, 0.5) * block_levels(key_list[6], (PARALLEL_COUNT, MERIDIAN_COUNT), ((0, 4), (1, 8)), -0.4, 0.0), -0.5, 0.5)
    return {"heat_content": heat_content, "saltiness_anomaly": saltiness_anomaly, "water_indicator": water_indicator, "gradient_kind_index": gradient_kind_index, "gradient_kind_table": gradient_kind_table, "easterly_transit_number": easterly_transit_number, "poleward_transit_number": poleward_transit_number}


def face_flux_terms(far_left_tracer, lower_tracer, upper_tracer, far_right_tracer, lower_tracer_northern, upper_tracer_northern, lower_tracer_southern, upper_tracer_southern, lower_mask, upper_mask, lower_velocity, upper_velocity, lower_slope_first, upper_slope_first, lower_slope_second, upper_slope_second):
    face_velocity = 0.5 * (lower_velocity + upper_velocity)
    downwind_value = upper_tracer - lower_tracer
    forward = face_velocity > 0
    du = jnp.where(forward, lower_tracer - far_left_tracer, far_right_tracer - upper_tracer)
    lim = jnp.where(downwind_value * du > 0, jnp.where(jnp.abs(downwind_value) < jnp.abs(du), downwind_value, du), 0.0)
    face_value = jnp.where(forward, lower_tracer, upper_tracer) + jnp.where(forward, 0.5, -0.5) * (1.0 - jnp.abs(face_velocity)) * lim
    first_slope = 0.5 * (lower_slope_first + upper_slope_first)
    second_slope = 0.5 * (lower_slope_second + upper_slope_second)
    cross_terms = 0.25 * (lower_tracer_northern + upper_tracer_northern - lower_tracer_southern - upper_tracer_southern)
    return lower_mask * upper_mask * (0.1 * ((1.0 + first_slope * first_slope) * downwind_value + first_slope * second_slope * cross_terms) - face_velocity * face_value)


def advance(ext, stat):
    rows = ext.shape[1] - 4
    cols = ext.shape[2] - 4

    def win(a, r0, c0, nr, nc):
        return a[..., r0:r0 + nr, c0:c0 + nc]

    def xs(a, r0, c0):
        return win(a, r0, c0, rows, cols + 1)

    def ys(a, r0, c0):
        return win(a, r0, c0, rows + 1, cols)

    sea_mask, easterly_isoneutral_gradient, poleward_isoneutral_gradient, u_vel, v_vel = stat[0], stat[1], stat[2], stat[3], stat[4]
    east = face_flux_terms(xs(ext, 2, 0), xs(ext, 2, 1), xs(ext, 2, 2), xs(ext, 2, 3),
                      xs(ext, 3, 1), xs(ext, 3, 2), xs(ext, 1, 1), xs(ext, 1, 2),
                      xs(sea_mask, 2, 1), xs(sea_mask, 2, 2), xs(u_vel, 2, 1), xs(u_vel, 2, 2),
                      xs(easterly_isoneutral_gradient, 2, 1), xs(easterly_isoneutral_gradient, 2, 2), xs(poleward_isoneutral_gradient, 2, 1), xs(poleward_isoneutral_gradient, 2, 2))
    north = face_flux_terms(ys(ext, 0, 2), ys(ext, 1, 2), ys(ext, 2, 2), ys(ext, 3, 2),
                       ys(ext, 1, 3), ys(ext, 2, 3), ys(ext, 1, 1), ys(ext, 2, 1),
                       ys(sea_mask, 1, 2), ys(sea_mask, 2, 2), ys(v_vel, 1, 2), ys(v_vel, 2, 2),
                       ys(poleward_isoneutral_gradient, 1, 2), ys(poleward_isoneutral_gradient, 2, 2), ys(easterly_isoneutral_gradient, 1, 2), ys(easterly_isoneutral_gradient, 2, 2))
    centre = win(ext, 2, 2, rows, cols)
    sea = win(sea_mask, 2, 2, rows, cols)
    return sea * (centre + east[..., 1:] - east[..., :-1] + north[..., 1:, :] - north[..., :-1, :])


def extend_global(stacked_fields, signs):
    sign_arr = jnp.array(signs, jnp.float32)[:, None, None]
    nrows = stacked_fields.shape[1]
    ghost = stacked_fields[:, nrows - 2:, :][:, ::-1, ::-1] * sign_arr
    south = jnp.zeros((stacked_fields.shape[0], 2, stacked_fields.shape[2]), jnp.float32)
    ext = jnp.concatenate([south, stacked_fields, ghost], 1)
    return jnp.concatenate([ext[..., -2:], ext, ext[..., :2]], 2)


def reference(heat_content, saltiness_anomaly, water_indicator, gradient_kind_index, gradient_kind_table, easterly_transit_number, poleward_transit_number):
    sea_mask = water_indicator.astype(jnp.float32)
    easterly_isoneutral_gradient = gradient_kind_table[:, 0][gradient_kind_index]
    poleward_isoneutral_gradient = gradient_kind_table[:, 1][gradient_kind_index]
    static = jnp.stack([sea_mask, easterly_isoneutral_gradient, poleward_isoneutral_gradient, easterly_transit_number, poleward_transit_number])
    stat = extend_global(static, (1.0, 1.0, 1.0, -1.0, -1.0))
    transported_quantities = jnp.stack([heat_content, saltiness_anomaly])
    for step in range(STEPS):
        transported_quantities = advance(extend_global(transported_quantities, (1.0, 1.0)), stat)
    return transported_quantities[0], transported_quantities[1]
```

```python
import functools

import jax
import jax.numpy as jnp
from jax import lax
from jax.experimental import pallas as pl
from jax.experimental.pallas import tpu as pltpu
from jax.sharding import PartitionSpec as P

STEPS = 4
HALO = 2 * STEPS
FIELDS = 6
LANES = 128
PAD = 8
BASE = PAD + HALO
PACKED = FIELDS * HALO
HALF = 64
MESH = pl.DeviceIdType.MESH


def lane_index(rows=8):
    return lax.broadcasted_iota(jnp.int32, (rows, LANES), 1)


def kernel(
    nlat, nlon,
    t_in, s_in, m_in, k_in, table, u_in, v_in,
    t_out, s_out,
    ext, qb, ints, slope, coef, gy,
    pack, pack_t, tops, bots,
    col_t, nbuf, sbuf, corner, comb,
    load_sem, send_sem, recv_sem,
):
    rows, cols = t_in.shape
    own = cols // LANES
    nt = own + 1
    lat = lax.axis_index("lat")
    lon = lax.axis_index("lon")
    top = lat == nlat - 1
    low = lat == 0
    east = lax.rem(lon + 1, nlon)
    west = lax.rem(lon + nlon - 1, nlon)
    fold = nlon - 1 - lon
    fold_e = lax.rem(2 * nlon - 2 - lon, nlon)
    fold_w = lax.rem(nlon - lon, nlon)

    loads = []
    for f, ref in enumerate((t_in, s_in, u_in, v_in)):
        for t in range(own):
            loads.append(pltpu.make_async_copy(
                ref.at[:, pl.ds(LANES * t, LANES)],
                ext.at[f, t, pl.ds(BASE, rows), :],
                load_sem.at[len(loads)]))
    for f, ref in enumerate((m_in, k_in)):
        for t in range(own):
            loads.append(pltpu.make_async_copy(
                ref.at[:, pl.ds(LANES * t, LANES)],
                ints.at[f, t],
                load_sem.at[len(loads)]))
    for c in loads:
        c.start()

    barrier = pltpu.get_barrier_semaphore()

    def greet(a, o):
        pl.semaphore_signal(barrier, inc=1, device_id=(o, a), device_id_type=MESH)

    greet(lat, east)
    greet(lat, west)

    @pl.when(jnp.logical_not(top))
    def _():
        greet(lat + 1, lon)
        greet(lat + 1, east)
        greet(lat + 1, west)

    @pl.when(jnp.logical_not(low))
    def _():
        greet(lat - 1, lon)
        greet(lat - 1, east)
        greet(lat - 1, west)

    @pl.when(top)
    def _():
        greet(lat, fold)

        @pl.when(fold_e != lon)
        def _():
            greet(lat, fold_e)

        @pl.when(fold_w != lon)
        def _():
            greet(lat, fold_w)

    for c in loads:
        c.wait()

    lane = lane_index()

    def pack_rows(i, _):
        r = pl.multiple_of(i * 8, 8)
        out = jnp.zeros((8, LANES), jnp.float32)
        for f in range(FIELDS):
            if f < 4:
                first = ext[f, 0, pl.ds(BASE + r, 8), :]
                last = ext[f, own - 1, pl.ds(BASE + r, 8), :]
            else:
                parts = [ints[f - 4, t, pl.ds(r, 8), :].astype(jnp.float32) for t in range(own)]
                for t in range(own):
                    ext[f, t, pl.ds(BASE + r, 8), :] = parts[t]
                first, last = parts[0], parts[-1]
            a = HALO * f
            b = HALF + HALO * f
            out = jnp.where((lane >= a) & (lane < a + HALO),
                            pltpu.roll(first, a, 1) if a else first, out)
            out = jnp.where((lane >= b) & (lane < b + HALO),
                            pltpu.roll(last, (b - (LANES - HALO)) % LANES, 1), out)
        pack[pl.ds(r, 8), :] = out
        return 0

    lax.fori_loop(0, rows // 8, pack_rows, 0)
    for h in range(rows // LANES):
        pack_t[:, pl.ds(LANES * h, LANES)] = pack[pl.ds(LANES * h, LANES), :].T
    for f in range(FIELDS):
        for t in range(own):
            tops[pl.ds(8 * f, 8), pl.ds(LANES * t, LANES)] = ext[f, t, pl.ds(BASE + rows - 8, 8), :]
            bots[pl.ds(8 * f, 8), pl.ds(LANES * t, LANES)] = ext[f, t, pl.ds(BASE, 8), :]

    others = lambda x: jnp.where(x, 1, 0)
    count = 2 + 3 * others(jnp.logical_not(low)) + others(top) * (
        1 + others(fold_e != lon) + others(fold_w != lon)) + 3 * others(jnp.logical_not(top))
    pl.semaphore_wait(barrier, count)

    pack_top = pack.at[pl.ds(rows - 8, 8), :]
    pack_low = pack.at[pl.ds(0, 8), :]
    from_west = col_t.at[pl.ds(HALF, PACKED), :]
    from_east = col_t.at[pl.ds(0, PACKED), :]

    def rdma(src, dst, s, r, a, o):
        return pltpu.make_async_remote_copy(
            src_ref=src, dst_ref=dst, send_sem=send_sem.at[s], recv_sem=recv_sem.at[r],
            device_id=(o, a), device_id_type=MESH)

    to_east = rdma(pack_t.at[pl.ds(HALF, PACKED), :], from_west, 0, 0, lat, east)
    to_west = rdma(pack_t.at[pl.ds(0, PACKED), :], from_east, 1, 1, lat, west)
    north = [
        rdma(tops, sbuf, 2, 3, lat + 1, lon),
        rdma(pack_top, corner.at[1], 3, 5, lat + 1, east),
        rdma(pack_top, corner.at[0], 4, 4, lat + 1, west),
    ]
    mirror = rdma(tops, nbuf, 2, 2, lat, fold)
    mirror_e = rdma(pack_top, corner.at[2], 3, 6, lat, fold_e)
    mirror_w = rdma(pack_top, corner.at[3], 4, 7, lat, fold_w)
    south = [
        rdma(bots, nbuf, 5, 2, lat - 1, lon),
        rdma(pack_low, corner.at[3], 6, 7, lat - 1, east),
        rdma(pack_low, corner.at[2], 7, 6, lat - 1, west),
    ]

    to_east.start()
    to_west.start()

    @pl.when(top)
    def _():
        mirror.start()

        @pl.when(fold_e != lon)
        def _():
            mirror_e.start()

        @pl.when(fold_w != lon)
        def _():
            mirror_w.start()

        @pl.when(fold_e == lon)
        def _():
            corner[2] = pack[pl.ds(rows - 8, 8), :]

        @pl.when(fold_w == lon)
        def _():
            corner[3] = pack[pl.ds(rows - 8, 8), :]

    @pl.when(jnp.logical_not(top))
    def _():
        for c in north:
            c.start()

    @pl.when(jnp.logical_not(low))
    def _():
        for c in south:
            c.start()

    nclass = table.shape[0]

    def slopes(idx):
        res = []
        for d in range(2):
            vals = [table[k, d] for k in range(nclass)]
            bit = 1
            while len(vals) > 1:
                on = (idx & bit) != 0
                vals = [jnp.where(on, vals[j + 1], vals[j]) if j + 1 < len(vals) else vals[j]
                        for j in range(0, len(vals), 2)]
                bit *= 2
            res.append(vals[0])
        return res

    def own_slopes(i, _):
        r = pl.multiple_of(i * 8, 8)
        for t in range(own):
            a, b = slopes(ints[1, t, pl.ds(r, 8), :])
            slope[0, t, pl.ds(BASE + r, 8), :] = a
            slope[1, t, pl.ds(BASE + r, 8), :] = b
        return 0

    lax.fori_loop(0, rows // 8, own_slopes, 0)

    to_east.wait_recv()
    to_west.wait_recv()
    for h in range(rows // LANES):
        comb[pl.ds(HALO + LANES * h, LANES), :] = col_t[:, pl.ds(LANES * h, LANES)].T

    @pl.when(low)
    def _():
        comb[pl.ds(0, 8), :] = jnp.zeros((8, LANES), jnp.float32)
        for f in range(FIELDS):
            for t in range(own):
                ext[f, t, pl.ds(PAD, 8), :] = jnp.zeros((8, LANES), jnp.float32)

    @pl.when(jnp.logical_not(low))
    def _():
        north[0].wait_recv()
        north[1].wait_recv()
        north[2].wait_recv()
        comb[pl.ds(0, 8), :] = jnp.where(lane < HALF, corner[0], corner[1])
        for f in range(FIELDS):
            for t in range(own):
                ext[f, t, pl.ds(PAD, 8), :] = sbuf[pl.ds(8 * f, 8), pl.ds(LANES * t, LANES)]

    mirror.wait_recv()

    @pl.when(jnp.logical_not(top))
    def _():
        mirror_e.wait_recv()
        mirror_w.wait_recv()
        comb[pl.ds(HALO + rows, 8), :] = jnp.where(lane < HALF, corner[2], corner[3])
        for f in range(FIELDS):
            for t in range(own):
                ext[f, t, pl.ds(BASE + rows, 8), :] = nbuf[pl.ds(8 * f, 8), pl.ds(LANES * t, LANES)]

    @pl.when(top)
    def _():
        @pl.when(fold_e != lon)
        def _():
            mirror_e.wait_recv()

        @pl.when(fold_w != lon)
        def _():
            mirror_w.wait_recv()

        def dot(a, b):
            return jnp.dot(a, b, precision=lax.Precision.HIGHEST, preferred_element_type=jnp.float32)

        def iotas(n):
            return (lax.broadcasted_iota(jnp.int32, (n, n), 0), lax.broadcasted_iota(jnp.int32, (n, n), 1))

        i, j = iotas(cols)
        flip = jnp.where(i + j == cols - 1, 1.0, 0.0)
        i, j = iotas(PACKED)
        turn = jnp.where(j == i + 7 - 2 * (i & 7), 1.0, 0.0)
        turned = dot(turn, dot(nbuf[...], flip))
        for f in range(FIELDS):
            sign = -1.0 if f in (2, 3) else 1.0
            for t in range(own):
                ext[f, t, pl.ds(BASE + rows, 8), :] = sign * turned[8 * f:8 * f + 8, LANES * t:LANES * t + LANES]
        i, j = iotas(LANES)
        swap = jnp.where(i == ((j + HALF) & 127) + 7 - 2 * (j & 7), 1.0, 0.0)
        i, j = iotas(8)
        turn8 = jnp.where(i + j == 7, 1.0, 0.0)
        mixed = jnp.where(lane >= HALF, corner[2], corner[3])
        mixed = dot(turn8, dot(mixed, swap))
        flipped = ((lane & 63) >= 2 * HALO) & ((lane & 63) < 4 * HALO)
        comb[pl.ds(HALO + rows, 8), :] = jnp.where(flipped, -mixed, mixed)

    def unpack(i, _):
        r = pl.multiple_of(i * 8, 8)
        both = comb[pl.ds(r, 8), :]
        for f in range(FIELDS):
            a = pltpu.roll(both, (-HALO * f) % LANES, 1) if f else both
            b = pltpu.roll(both, (LANES - HALO - HALF - HALO * f) % LANES, 1)
            third = jnp.where(lane < HALF, a, b)
            if f < 5:
                ext[f, own, pl.ds(PAD + r, 8), :] = third
            else:
                a, b = slopes(third.astype(jnp.int32))
                slope[0, own, pl.ds(PAD + r, 8), :] = a
                slope[1, own, pl.ds(PAD + r, 8), :] = b
        return 0

    chunks = (rows + 2 * HALO) // 8
    lax.fori_loop(0, chunks, unpack, 0)
    for t in range(own):
        for r in (PAD, BASE + rows):
            a, b = slopes(ext[5, t, pl.ds(r, 8), :].astype(jnp.int32))
            slope[0, t, pl.ds(r, 8), :] = a
            slope[1, t, pl.ds(r, 8), :] = b

    def shift_east(x):
        r = [pltpu.roll(a, LANES - 1, 1) for a in x]
        return [jnp.where(lane == LANES - 1, r[(t + 1) % nt], r[t]) for t in range(nt)]

    def shift_west(x):
        r = [pltpu.roll(a, 1, 1) for a in x]
        return [jnp.where(lane == 0, r[t - 1], r[t]) for t in range(nt)]

    def rows_of(ref, f, r):
        return [ref[f, t, pl.ds(r, 8), :] for t in range(nt)]

    def coefs(i, _):
        r = pl.multiple_of(PAD + i * 8, 8)
        m0, u0, v0 = rows_of(ext, 4, r), rows_of(ext, 2, r), rows_of(ext, 3, r)
        x0, y0 = rows_of(slope, 0, r), rows_of(slope, 1, r)
        m1, v1 = rows_of(ext, 4, r + 1), rows_of(ext, 3, r + 1)
        x1, y1 = rows_of(slope, 0, r + 1), rows_of(slope, 1, r + 1)
        me, ue, xe, ye = shift_east(m0), shift_east(u0), shift_east(x0), shift_east(y0)
        for t in range(nt):
            for d, (ma, mb, wa, wb, aa, ab, ba, bb) in enumerate((
                    (m0, me, u0, ue, x0, xe, y0, ye),
                    (m0, m1, v0, v1, y0, y1, x0, x1))):
                m = ma[t] * mb[t]
                vel = 0.5 * (wa[t] + wb[t])
                sa = 0.5 * (aa[t] + ab[t])
                sb = 0.5 * (ba[t] + bb[t])
                speed = jnp.abs(vel)
                coef[4 * d, t, pl.ds(r, 8), :] = m * (0.1 * (1.0 + sa * sa) - jnp.minimum(vel, 0.0))
                coef[4 * d + 1, t, pl.ds(r, 8), :] = m * (0.025 * (sa * sb))
                coef[4 * d + 2, t, pl.ds(r, 8), :] = m * vel
                coef[4 * d + 3, t, pl.ds(r, 8), :] = m * (0.5 * speed * (1.0 - speed))
        return 0

    lax.fori_loop(0, chunks, coefs, 0)

    def limited(dn, du):
        return jnp.maximum(jnp.minimum(dn, du), jnp.minimum(jnp.maximum(dn, du), 0.0))

    def stepped(src, f, r, masked, k):
        qm, q0, q1, q2 = [rows_of(src, f, r + j) for j in (-1, 0, 1, 2)]
        ts = range(nt)
        qe = shift_east(q0)
        dn = [qe[t] - q0[t] for t in ts]
        dw, de = shift_west(dn), shift_east(dn)
        vert = [q1[t] - qm[t] for t in ts]
        ve = shift_east(vert)
        gx = []
        for t in ts:
            lim = limited(dn[t], jnp.where(k[2][t] > 0, dw[t], de[t]))
            gx.append(k[0][t] * dn[t] + k[1][t] * (vert[t] + ve[t]) - (k[2][t] * q0[t] + k[3][t] * lim))
        gw = shift_west(gx)
        pair = [q0[t] + q1[t] for t in ts]
        pe, pw = shift_east(pair), shift_west(pair)
        new = []
        for t in ts:
            dn = q1[t] - q0[t]
            lim = limited(dn, jnp.where(k[6][t] > 0, q0[t] - qm[t], q2[t] - q1[t]))
            g = k[4][t] * dn + k[5][t] * (pe[t] - pw[t]) - (k[6][t] * q0[t] + k[7][t] * lim)
            gy[f, t, pl.ds(r, 8), :] = g
            centre = q0[t] * masked[t] if masked is not None else q0[t]
            new.append(centre + (gx[t] - gw[t]) + g)
        return [new[t] - gy[f, t, pl.ds(r - 1, 8), :] for t in ts]

    def advance(step, src, dst, r):
        k = [rows_of(coef, j, r) for j in range(8)]
        masked = rows_of(ext, 4, r) if step == 0 else None
        for f in range(2):
            new = stepped(src, f, r, masked, k)
            if step < STEPS - 1:
                for t in range(nt):
                    dst[f, t, pl.ds(r, 8), :] = new[t]
            else:
                out = (t_out, s_out)[f]
                for t in range(own):
                    out[pl.ds(pl.multiple_of(r - BASE, 8), 8), pl.ds(LANES * t, LANES)] = new[t]

    pairs = ((ext, qb), (qb, ext))
    for step in range(STEPS):
        src, dst = pairs[step % 2]
        if step < STEPS - 1:
            def body(i, _, step=step, src=src, dst=dst):
                advance(step, src, dst, pl.multiple_of(PAD + i * 8, 8))
                return 0
            lax.fori_loop(0, chunks, body, 0)
        else:
            k = [rows_of(coef, j, PAD) for j in range(8)]
            for f in range(2):
                stepped(src, f, PAD, None, k)

            def body(i, _, step=step, src=src, dst=dst):
                advance(step, src, dst, pl.multiple_of(BASE + i * 8, 8))
                return 0
            lax.fori_loop(0, rows // 8, body, 0)

    to_east.wait_send()
    to_west.wait_send()

    @pl.when(top)
    def _():
        mirror.wait_send()

        @pl.when(fold_e != lon)
        def _():
            mirror_e.wait_send()

        @pl.when(fold_w != lon)
        def _():
            mirror_w.wait_send()

    @pl.when(jnp.logical_not(top))
    def _():
        for c in north:
            c.wait_send()

    @pl.when(jnp.logical_not(low))
    def _():
        for c in south:
            c.wait_send()


def local(nlat, nlon, *args):
    rows, cols = args[0].shape
    nt = cols // LANES + 1
    tall = rows + 2 * BASE
    f32 = jnp.float32
    any_ = pl.BlockSpec(memory_space=pl.ANY)
    vmem = pl.BlockSpec(memory_space=pltpu.VMEM)
    return pl.pallas_call(
        functools.partial(kernel, nlat, nlon),
        out_shape=(jax.ShapeDtypeStruct((rows, cols), f32),) * 2,
        in_specs=[any_, any_, any_, any_, pl.BlockSpec(memory_space=pltpu.SMEM), any_, any_],
        out_specs=(vmem, vmem),
        scratch_shapes=[
            pltpu.VMEM((FIELDS, nt, tall, LANES), f32),
            pltpu.VMEM((2, nt, tall, LANES), f32),
            pltpu.VMEM((2, nt - 1, rows, LANES), jnp.int32),
            pltpu.VMEM((2, nt, tall, LANES), f32),
            pltpu.VMEM((8, nt, tall, LANES), f32),
            pltpu.VMEM((2, nt, tall, LANES), f32),
            pltpu.VMEM((rows, LANES), f32),
            pltpu.VMEM((LANES, rows), f32),
            pltpu.VMEM((PACKED, cols), f32),
            pltpu.VMEM((PACKED, cols), f32),
            pltpu.VMEM((LANES, rows), f32),
            pltpu.VMEM((PACKED, cols), f32),
            pltpu.VMEM((PACKED, cols), f32),
            pltpu.VMEM((4, 8, LANES), f32),
            pltpu.VMEM((rows + 2 * HALO, LANES), f32),
            pltpu.SemaphoreType.DMA((FIELDS * (nt - 1),)),
            pltpu.SemaphoreType.DMA((8,)),
            pltpu.SemaphoreType.DMA((8,)),
        ],
        compiler_params=pltpu.CompilerParams(
            collective_id=0, has_side_effects=True, vmem_limit_bytes=48 * 1024 * 1024),
        name="tracer_steps",
    )(*args)


def solution(mesh):
    names = dict(zip(mesh.axis_names, mesh.devices.shape))
    block = P("lat", "lon")
    return jax.shard_map(
        functools.partial(local, names["lat"], names["lon"]),
        mesh=mesh,
        in_specs=(block, block, block, block, P(), block, block),
        out_specs=(block, block),
        check_vma=False,
    )
```

```python
import functools

import jax
import jax.numpy as jnp
from jax import lax
from jax.experimental import pallas as pl
from jax.experimental.pallas import tpu as pltpu
from jax.sharding import PartitionSpec as P

STEPS = 4
HALO = 2 * STEPS
FIELDS = 6
LANES = 128
PAD = 8
BASE = PAD + HALO
PACKED = FIELDS * HALO
HALF = 64
MESH = pl.DeviceIdType.MESH


GROUP = 4


def over_chunks(count, group, body):
    def some(i, _):
        body([i * group + j for j in range(group)])
        return 0

    lax.fori_loop(0, count // group, some, 0)
    if count % group:
        body(list(range(count - count % group, count)))


def each(body):
    def run(group):
        for i in group:
            body(i)

    return run


def row_of(r):
    return r if isinstance(r, int) else pl.multiple_of(r, 8)


def lane_index(rows=8):
    return lax.broadcasted_iota(jnp.int32, (rows, LANES), 1)


def kernel(
    nlat, nlon,
    t_in, s_in, m_in, k_in, table, u_in, v_in,
    t_out, s_out,
    ext, qb, ints, slope, coef, gy,
    pack, pack_t, tops, bots,
    col_t, nbuf, sbuf, corner, comb,
    load_sem, send_sem, recv_sem,
):
    rows, cols = t_in.shape
    own = cols // LANES
    nt = own + 1
    lat = lax.axis_index("lat")
    lon = lax.axis_index("lon")
    top = lat == nlat - 1
    low = lat == 0
    east = lax.rem(lon + 1, nlon)
    west = lax.rem(lon + nlon - 1, nlon)
    fold = nlon - 1 - lon
    fold_e = lax.rem(2 * nlon - 2 - lon, nlon)
    fold_w = lax.rem(nlon - lon, nlon)

    loads = []
    for f, ref in enumerate((t_in, s_in, u_in, v_in)):
        for t in range(own):
            loads.append(pltpu.make_async_copy(
                ref.at[:, pl.ds(LANES * t, LANES)],
                ext.at[f, t, pl.ds(BASE, rows), :],
                load_sem.at[len(loads)]))
    for f, ref in enumerate((m_in, k_in)):
        for t in range(own):
            loads.append(pltpu.make_async_copy(
                ref.at[:, pl.ds(LANES * t, LANES)],
                ints.at[f, t],
                load_sem.at[len(loads)]))
    for c in loads:
        c.start()

    barrier = pltpu.get_barrier_semaphore()

    def greet(a, o):
        pl.semaphore_signal(barrier, inc=1, device_id=(o, a), device_id_type=MESH)

    greet(lat, east)
    greet(lat, west)

    @pl.when(jnp.logical_not(top))
    def _():
        greet(lat + 1, lon)
        greet(lat + 1, east)
        greet(lat + 1, west)

    @pl.when(jnp.logical_not(low))
    def _():
        greet(lat - 1, lon)
        greet(lat - 1, east)
        greet(lat - 1, west)

    @pl.when(top)
    def _():
        greet(lat, fold)

        @pl.when(fold_e != lon)
        def _():
            greet(lat, fold_e)

        @pl.when(fold_w != lon)
        def _():
            greet(lat, fold_w)

    for c in loads:
        c.wait()

    lane = lane_index()

    def pack_rows(i):
        r = row_of(i * 8)
        out = jnp.zeros((8, LANES), jnp.float32)
        for f in range(FIELDS):
            if f < 4:
                first = ext[f, 0, pl.ds(BASE + r, 8), :]
                last = ext[f, own - 1, pl.ds(BASE + r, 8), :]
            else:
                parts = [ints[f - 4, t, pl.ds(r, 8), :].astype(jnp.float32) for t in range(own)]
                for t in range(own):
                    ext[f, t, pl.ds(BASE + r, 8), :] = parts[t]
                first, last = parts[0], parts[-1]
            a = HALO * f
            b = HALF + HALO * f
            out = jnp.where((lane >= a) & (lane < a + HALO),
                            pltpu.roll(first, a, 1) if a else first, out)
            out = jnp.where((lane >= b) & (lane < b + HALO),
                            pltpu.roll(last, (b - (LANES - HALO)) % LANES, 1), out)
        pack[pl.ds(r, 8), :] = out

    over_chunks(rows // 8, GROUP, each(pack_rows))
    for h in range(rows // LANES):
        pack_t[:, pl.ds(LANES * h, LANES)] = pack[pl.ds(LANES * h, LANES), :].T
    for f in range(FIELDS):
        for t in range(own):
            tops[pl.ds(8 * f, 8), pl.ds(LANES * t, LANES)] = ext[f, t, pl.ds(BASE + rows - 8, 8), :]
            bots[pl.ds(8 * f, 8), pl.ds(LANES * t, LANES)] = ext[f, t, pl.ds(BASE, 8), :]

    others = lambda x: jnp.where(x, 1, 0)
    count = 2 + 3 * others(jnp.logical_not(low)) + others(top) * (
        1 + others(fold_e != lon) + others(fold_w != lon)) + 3 * others(jnp.logical_not(top))
    pl.semaphore_wait(barrier, count)

    pack_top = pack.at[pl.ds(rows - 8, 8), :]
    pack_low = pack.at[pl.ds(0, 8), :]
    from_west = col_t.at[pl.ds(HALF, PACKED), :]
    from_east = col_t.at[pl.ds(0, PACKED), :]

    def rdma(src, dst, s, r, a, o):
        return pltpu.make_async_remote_copy(
            src_ref=src, dst_ref=dst, send_sem=send_sem.at[s], recv_sem=recv_sem.at[r],
            device_id=(o, a), device_id_type=MESH)

    to_east = rdma(pack_t.at[pl.ds(HALF, PACKED), :], from_west, 0, 0, lat, east)
    to_west = rdma(pack_t.at[pl.ds(0, PACKED), :], from_east, 1, 1, lat, west)
    north = [
        rdma(tops, sbuf, 2, 3, lat + 1, lon),
        rdma(pack_top, corner.at[1], 3, 5, lat + 1, east),
        rdma(pack_top, corner.at[0], 4, 4, lat + 1, west),
    ]
    mirror = rdma(tops, nbuf, 2, 2, lat, fold)
    mirror_e = rdma(pack_top, corner.at[2], 3, 6, lat, fold_e)
    mirror_w = rdma(pack_top, corner.at[3], 4, 7, lat, fold_w)
    south = [
        rdma(bots, nbuf, 5, 2, lat - 1, lon),
        rdma(pack_low, corner.at[3], 6, 7, lat - 1, east),
        rdma(pack_low, corner.at[2], 7, 6, lat - 1, west),
    ]

    to_east.start()
    to_west.start()

    @pl.when(top)
    def _():
        mirror.start()

        @pl.when(fold_e != lon)
        def _():
            mirror_e.start()

        @pl.when(fold_w != lon)
        def _():
            mirror_w.start()

        @pl.when(fold_e == lon)
        def _():
            corner[2] = pack[pl.ds(rows - 8, 8), :]

        @pl.when(fold_w == lon)
        def _():
            corner[3] = pack[pl.ds(rows - 8, 8), :]

    @pl.when(jnp.logical_not(top))
    def _():
        for c in north:
            c.start()

    @pl.when(jnp.logical_not(low))
    def _():
        for c in south:
            c.start()

    nclass = table.shape[1]

    def slopes(idx):
        res = []
        for d in range(2):
            vals = [table[d, k] for k in range(nclass)]
            bit = 1
            while len(vals) > 1:
                on = (idx & bit) != 0
                vals = [jnp.where(on, vals[j + 1], vals[j]) if j + 1 < len(vals) else vals[j]
                        for j in range(0, len(vals), 2)]
                bit *= 2
            res.append(vals[0])
        return res

    def own_slopes(i):
        r = row_of(i * 8)
        for t in range(own):
            a, b = slopes(ints[1, t, pl.ds(r, 8), :])
            slope[0, t, pl.ds(BASE + r, 8), :] = a
            slope[1, t, pl.ds(BASE + r, 8), :] = b

    over_chunks(rows // 8, GROUP, each(own_slopes))

    to_east.wait_recv()
    to_west.wait_recv()
    for h in range(rows // LANES):
        comb[pl.ds(HALO + LANES * h, LANES), :] = col_t[:, pl.ds(LANES * h, LANES)].T

    @pl.when(low)
    def _():
        comb[pl.ds(0, 8), :] = jnp.zeros((8, LANES), jnp.float32)
        for f in range(FIELDS):
            for t in range(own):
                ext[f, t, pl.ds(PAD, 8), :] = jnp.zeros((8, LANES), jnp.float32)

    @pl.when(jnp.logical_not(low))
    def _():
        north[0].wait_recv()
        north[1].wait_recv()
        north[2].wait_recv()
        comb[pl.ds(0, 8), :] = jnp.where(lane < HALF, corner[0], corner[1])
        for f in range(FIELDS):
            for t in range(own):
                ext[f, t, pl.ds(PAD, 8), :] = sbuf[pl.ds(8 * f, 8), pl.ds(LANES * t, LANES)]

    mirror.wait_recv()

    @pl.when(jnp.logical_not(top))
    def _():
        mirror_e.wait_recv()
        mirror_w.wait_recv()
        comb[pl.ds(HALO + rows, 8), :] = jnp.where(lane < HALF, corner[2], corner[3])
        for f in range(FIELDS):
            for t in range(own):
                ext[f, t, pl.ds(BASE + rows, 8), :] = nbuf[pl.ds(8 * f, 8), pl.ds(LANES * t, LANES)]

    @pl.when(top)
    def _():
        @pl.when(fold_e != lon)
        def _():
            mirror_e.wait_recv()

        @pl.when(fold_w != lon)
        def _():
            mirror_w.wait_recv()

        def dot(a, b):
            return jnp.dot(a, b, precision=lax.Precision.HIGHEST, preferred_element_type=jnp.float32)

        def iotas(n):
            return (lax.broadcasted_iota(jnp.int32, (n, n), 0), lax.broadcasted_iota(jnp.int32, (n, n), 1))

        i, j = iotas(cols)
        flip = jnp.where(i + j == cols - 1, 1.0, 0.0)
        i, j = iotas(PACKED)
        turn = jnp.where(j == i + 7 - 2 * (i & 7), 1.0, 0.0)
        turned = dot(turn, dot(nbuf[...], flip))
        for f in range(FIELDS):
            sign = -1.0 if f in (2, 3) else 1.0
            for t in range(own):
                ext[f, t, pl.ds(BASE + rows, 8), :] = sign * turned[8 * f:8 * f + 8, LANES * t:LANES * t + LANES]
        i, j = iotas(LANES)
        swap = jnp.where(i == ((j + HALF) & 127) + 7 - 2 * (j & 7), 1.0, 0.0)
        i, j = iotas(8)
        turn8 = jnp.where(i + j == 7, 1.0, 0.0)
        mixed = jnp.where(lane >= HALF, corner[2], corner[3])
        mixed = dot(turn8, dot(mixed, swap))
        flipped = ((lane & 63) >= 2 * HALO) & ((lane & 63) < 4 * HALO)
        comb[pl.ds(HALO + rows, 8), :] = jnp.where(flipped, -mixed, mixed)

    def unpack(i):
        r = row_of(i * 8)
        both = comb[pl.ds(r, 8), :]
        for f in range(FIELDS):
            a = pltpu.roll(both, (-HALO * f) % LANES, 1) if f else both
            b = pltpu.roll(both, (LANES - HALO - HALF - HALO * f) % LANES, 1)
            third = jnp.where(lane < HALF, a, b)
            if f < 5:
                ext[f, own, pl.ds(PAD + r, 8), :] = third
            else:
                a, b = slopes(third.astype(jnp.int32))
                slope[0, own, pl.ds(PAD + r, 8), :] = a
                slope[1, own, pl.ds(PAD + r, 8), :] = b

    chunks = (rows + 2 * HALO) // 8
    over_chunks(chunks, GROUP, each(unpack))
    for t in range(own):
        for r in (PAD, BASE + rows):
            a, b = slopes(ext[5, t, pl.ds(r, 8), :].astype(jnp.int32))
            slope[0, t, pl.ds(r, 8), :] = a
            slope[1, t, pl.ds(r, 8), :] = b

    def shift_east(x):
        r = [pltpu.roll(a, LANES - 1, 1) for a in x]
        return [jnp.where(lane == LANES - 1, r[(t + 1) % nt], r[t]) for t in range(nt)]

    def shift_west(x):
        r = [pltpu.roll(a, 1, 1) for a in x]
        return [jnp.where(lane == 0, r[t - 1], r[t]) for t in range(nt)]

    def rows_of(ref, f, r):
        return [ref[f, t, pl.ds(r, 8), :] for t in range(nt)]

    def coefs(i):
        r = row_of(PAD + i * 8)
        m0, u0, v0 = rows_of(ext, 4, r), rows_of(ext, 2, r), rows_of(ext, 3, r)
        x0, y0 = rows_of(slope, 0, r), rows_of(slope, 1, r)
        m1, v1 = rows_of(ext, 4, r + 1), rows_of(ext, 3, r + 1)
        x1, y1 = rows_of(slope, 0, r + 1), rows_of(slope, 1, r + 1)
        me, ue, xe, ye = shift_east(m0), shift_east(u0), shift_east(x0), shift_east(y0)
        for t in range(nt):
            for d, (ma, mb, wa, wb, aa, ab, ba, bb) in enumerate((
                    (m0, me, u0, ue, x0, xe, y0, ye),
                    (m0, m1, v0, v1, y0, y1, x0, x1))):
                m = ma[t] * mb[t]
                vel = 0.5 * (wa[t] + wb[t])
                sa = 0.5 * (aa[t] + ab[t])
                sb = 0.5 * (ba[t] + bb[t])
                speed = jnp.abs(vel)
                coef[4 * d, t, pl.ds(r, 8), :] = m * (0.1 * (1.0 + sa * sa) - jnp.minimum(vel, 0.0))
                coef[4 * d + 1, t, pl.ds(r, 8), :] = m * (0.025 * (sa * sb))
                coef[4 * d + 2, t, pl.ds(r, 8), :] = m * vel
                coef[4 * d + 3, t, pl.ds(r, 8), :] = m * (0.5 * speed * (1.0 - speed))

    over_chunks(chunks, GROUP, each(coefs))

    def limited(dn, du):
        return jnp.maximum(jnp.minimum(dn, du), jnp.minimum(jnp.maximum(dn, du), 0.0))

    def shift_two(x):
        r = [pltpu.roll(a, LANES - 2, 1) for a in x]
        return [jnp.where(lane >= LANES - 2, r[(t + 1) % nt], r[t]) for t in range(nt)]

    def lat_flux(f, r, k, qm, q0, q1, q2, pe, pw, t):
        dn = q1[t] - q0[t]
        lim = limited(dn, jnp.where(k[2][t] > 0, q0[t] - qm[t], q2[t] - q1[t]))
        g = k[0][t] * dn + k[1][t] * (pe[t] - pw[t]) - (k[2][t] * q0[t] + k[3][t] * lim)
        gy[f, t, pl.ds(r, 8), :] = g
        return g

    def stepped(src, f, r, masked, k, keep):
        qm, q0, q1, q2 = [rows_of(src, f, r + j) for j in (-1, 0, 1, 2)]
        ts = range(nt)
        qe, qw, qf = shift_east(q0), shift_west(q0), shift_two(q0)
        vert = [q1[t] - qm[t] for t in ts]
        ve = shift_east(vert)
        pair = [q0[t] + q1[t] for t in ts]
        pe, pw = shift_east(pair), shift_west(pair)
        gx = []
        for t in ts:
            dn = qe[t] - q0[t]
            lim = limited(dn, jnp.where(k[2][t] > 0, q0[t] - qw[t], qf[t] - qe[t]))
            gx.append(k[0][t] * dn + k[1][t] * (vert[t] + ve[t]) - (k[2][t] * q0[t] + k[3][t] * lim))
        gw = shift_west(gx)
        new = []
        for t in range(keep):
            g = lat_flux(f, r, k[4:], qm, q0, q1, q2, pe, pw, t)
            centre = q0[t] * masked[t] if masked is not None else q0[t]
            new.append(centre + (gx[t] - gw[t]) + g)
        return new

    def advance(step, src, dst, first, group):
        last = step == STEPS - 1
        keep = own if last else nt
        found = []
        for i in group:
            r = row_of(first + i * 8)
            k = [rows_of(coef, j, r) for j in range(8)]
            masked = rows_of(ext, 4, r) if step == 0 else None
            for f in range(2):
                found.append((f, r, stepped(src, f, r, masked, k, keep)))
        for f, r, new in found:
            for t in range(keep):
                value = new[t] - gy[f, t, pl.ds(r - 1, 8), :]
                if last:
                    (t_out, s_out)[f][pl.ds(row_of(r - BASE), 8), pl.ds(LANES * t, LANES)] = value
                else:
                    dst[f, t, pl.ds(r, 8), :] = value

    pairs = ((ext, qb), (qb, ext))
    for step in range(STEPS):
        src, dst = pairs[step % 2]
        if step < STEPS - 1:
            over_chunks(chunks, GROUP, functools.partial(advance, step, src, dst, PAD))
        else:
            k = [rows_of(coef, j, PAD) for j in range(4, 8)]
            for f in range(2):
                qm, q0, q1, q2 = [rows_of(src, f, PAD + j) for j in (-1, 0, 1, 2)]
                pair = [q0[t] + q1[t] for t in range(nt)]
                pe, pw = shift_east(pair), shift_west(pair)
                for t in range(own):
                    lat_flux(f, PAD, k, qm, q0, q1, q2, pe, pw, t)
            over_chunks(rows // 8, GROUP, functools.partial(advance, step, src, dst, BASE))

    to_east.wait_send()
    to_west.wait_send()

    @pl.when(top)
    def _():
        mirror.wait_send()

        @pl.when(fold_e != lon)
        def _():
            mirror_e.wait_send()

        @pl.when(fold_w != lon)
        def _():
            mirror_w.wait_send()

    @pl.when(jnp.logical_not(top))
    def _():
        for c in north:
            c.wait_send()

    @pl.when(jnp.logical_not(low))
    def _():
        for c in south:
            c.wait_send()


def local(nlat, nlon, *args):
    rows, cols = args[0].shape
    nt = cols // LANES + 1
    tall = rows + 2 * BASE
    f32 = jnp.float32
    any_ = pl.BlockSpec(memory_space=pltpu.HBM)
    vmem = pl.BlockSpec(memory_space=pltpu.VMEM)
    return pl.pallas_call(
        functools.partial(kernel, nlat, nlon),
        out_shape=(jax.ShapeDtypeStruct((rows, cols), f32),) * 2,
        in_specs=[any_, any_, any_, any_, pl.BlockSpec(memory_space=pltpu.SMEM), any_, any_],
        out_specs=(vmem, vmem),
        scratch_shapes=[
            pltpu.VMEM((FIELDS, nt, tall, LANES), f32),
            pltpu.VMEM((2, nt, tall, LANES), f32),
            pltpu.VMEM((2, nt - 1, rows, LANES), jnp.int32),
            pltpu.VMEM((2, nt, tall, LANES), f32),
            pltpu.VMEM((8, nt, tall, LANES), f32),
            pltpu.VMEM((2, nt, tall, LANES), f32),
            pltpu.VMEM((rows, LANES), f32),
            pltpu.VMEM((LANES, rows), f32),
            pltpu.VMEM((PACKED, cols), f32),
            pltpu.VMEM((PACKED, cols), f32),
            pltpu.VMEM((LANES, rows), f32),
            pltpu.VMEM((PACKED, cols), f32),
            pltpu.VMEM((PACKED, cols), f32),
            pltpu.VMEM((4, 8, LANES), f32),
            pltpu.VMEM((rows + 2 * HALO, LANES), f32),
            pltpu.SemaphoreType.DMA((FIELDS * (nt - 1),)),
            pltpu.SemaphoreType.DMA((8,)),
            pltpu.SemaphoreType.DMA((8,)),
        ],
        compiler_params=pltpu.CompilerParams(
            collective_id=0, has_side_effects=True, vmem_limit_bytes=64 * 1024 * 1024 - 65536),
        name="tracer_steps",
    )(*args[:4], args[4].T, *args[5:])


def solution(mesh):
    names = dict(zip(mesh.axis_names, mesh.devices.shape))
    block = P("lat", "lon")
    return jax.shard_map(
        functools.partial(local, names["lat"], names["lon"]),
        mesh=mesh,
        in_specs=(block, block, block, block, P(), block, block),
        out_specs=(block, block),
        check_vma=False,
    )
```

```python
import functools

import jax
import jax.numpy as jnp
from jax import lax
from jax.experimental import pallas as pl
from jax.experimental.pallas import tpu as pltpu
from jax.sharding import PartitionSpec as P

STEPS = 4
HALO = 2 * STEPS
FIELDS = 6
LANES = 128
PAD = 8
BASE = PAD + HALO
PACKED = FIELDS * HALO
HALF = 64
MESH = pl.DeviceIdType.MESH


GROUP = 4
STRIP_GROUP = 17


def over_chunks(first, count, group, body):
    def some(i, _):
        body([first + i * group + j for j in range(group)])
        return 0

    lax.fori_loop(0, count // group, some, 0)
    if count % group:
        body([first + count - count % group + j for j in range(count % group)])


def each(body):
    def run(group):
        for i in group:
            body(i)

    return run


def row_of(r):
    return r if isinstance(r, int) else pl.multiple_of(r, 8)


def lane_index(rows=8):
    return lax.broadcasted_iota(jnp.int32, (rows, LANES), 1)


def kernel(
    nlat, nlon,
    t_in, s_in, m_in, k_in, table, u_in, v_in,
    t_out, s_out,
    q, stat, slope, ints, coef, gy,
    pack, pack_t, tops, bots,
    col_t, nbuf, sbuf, corner, comb,
    load_sem, send_sem, recv_sem,
):
    rows, cols = t_in.shape
    own = cols // LANES
    edge = own
    lat = lax.axis_index("lat")
    lon = lax.axis_index("lon")
    top = lat == nlat - 1
    low = lat == 0
    east = lax.rem(lon + 1, nlon)
    west = lax.rem(lon + nlon - 1, nlon)
    fold = nlon - 1 - lon
    fold_e = lax.rem(2 * nlon - 2 - lon, nlon)
    fold_w = lax.rem(nlon - lon, nlon)

    def field_at(f):
        return q.at[0, f] if f < 2 else stat.at[f - 2]

    loads = []
    for f, ref in enumerate((t_in, s_in, u_in, v_in)):
        for t in range(own):
            loads.append(pltpu.make_async_copy(
                ref.at[:, pl.ds(LANES * t, LANES)],
                field_at(f).at[t, pl.ds(BASE, rows), :],
                load_sem.at[len(loads)]))
    for f, ref in enumerate((m_in, k_in)):
        for t in range(own):
            loads.append(pltpu.make_async_copy(
                ref.at[:, pl.ds(LANES * t, LANES)],
                ints.at[f, t],
                load_sem.at[len(loads)]))
    for c in loads:
        c.start()

    barrier = pltpu.get_barrier_semaphore()

    def greet(a, o):
        pl.semaphore_signal(barrier, inc=1, device_id=(o, a), device_id_type=MESH)

    greet(lat, east)
    greet(lat, west)

    @pl.when(jnp.logical_not(top))
    def _():
        greet(lat + 1, lon)
        greet(lat + 1, east)
        greet(lat + 1, west)

    @pl.when(jnp.logical_not(low))
    def _():
        greet(lat - 1, lon)
        greet(lat - 1, east)
        greet(lat - 1, west)

    @pl.when(top)
    def _():
        greet(lat, fold)

        @pl.when(fold_e != lon)
        def _():
            greet(lat, fold_e)

        @pl.when(fold_w != lon)
        def _():
            greet(lat, fold_w)

    for c in loads:
        c.wait()

    lane = lane_index()

    def pack_rows(i):
        r = row_of(i * 8)
        out = jnp.zeros((8, LANES), jnp.float32)
        for f in range(FIELDS):
            if f < 4:
                first = field_at(f)[0, pl.ds(BASE + r, 8), :]
                last = field_at(f)[own - 1, pl.ds(BASE + r, 8), :]
            else:
                parts = [ints[f - 4, t, pl.ds(r, 8), :].astype(jnp.float32) for t in range(own)]
                for t in range(own):
                    field_at(f)[t, pl.ds(BASE + r, 8), :] = parts[t]
                first, last = parts[0], parts[-1]
            a = HALO * f
            b = HALF + HALO * f
            out = jnp.where((lane >= a) & (lane < a + HALO),
                            pltpu.roll(first, a, 1) if a else first, out)
            out = jnp.where((lane >= b) & (lane < b + HALO),
                            pltpu.roll(last, (b - (LANES - HALO)) % LANES, 1), out)
        pack[pl.ds(r, 8), :] = out

    over_chunks(0, rows // 8, GROUP, each(pack_rows))
    for h in range(rows // LANES):
        pack_t[:, pl.ds(LANES * h, LANES)] = pack[pl.ds(LANES * h, LANES), :].T
    for f in range(FIELDS):
        for t in range(own):
            tops[pl.ds(8 * f, 8), pl.ds(LANES * t, LANES)] = field_at(f)[t, pl.ds(BASE + rows - 8, 8), :]
            bots[pl.ds(8 * f, 8), pl.ds(LANES * t, LANES)] = field_at(f)[t, pl.ds(BASE, 8), :]

    others = lambda x: jnp.where(x, 1, 0)
    count = 2 + 3 * others(jnp.logical_not(low)) + others(top) * (
        1 + others(fold_e != lon) + others(fold_w != lon)) + 3 * others(jnp.logical_not(top))
    pl.semaphore_wait(barrier, count)

    pack_top = pack.at[pl.ds(rows - 8, 8), :]
    pack_low = pack.at[pl.ds(0, 8), :]
    from_west = col_t.at[pl.ds(HALF, PACKED), :]
    from_east = col_t.at[pl.ds(0, PACKED), :]

    def rdma(src, dst, s, r, a, o):
        return pltpu.make_async_remote_copy(
            src_ref=src, dst_ref=dst, send_sem=send_sem.at[s], recv_sem=recv_sem.at[r],
            device_id=(o, a), device_id_type=MESH)

    to_east = rdma(pack_t.at[pl.ds(HALF, PACKED), :], from_west, 0, 0, lat, east)
    to_west = rdma(pack_t.at[pl.ds(0, PACKED), :], from_east, 1, 1, lat, west)
    north = [
        rdma(tops, sbuf, 2, 3, lat + 1, lon),
        rdma(pack_top, corner.at[1], 3, 5, lat + 1, east),
        rdma(pack_top, corner.at[0], 4, 4, lat + 1, west),
    ]
    mirror = rdma(tops, nbuf, 2, 2, lat, fold)
    mirror_e = rdma(pack_top, corner.at[2], 3, 6, lat, fold_e)
    mirror_w = rdma(pack_top, corner.at[3], 4, 7, lat, fold_w)
    south = [
        rdma(bots, nbuf, 5, 2, lat - 1, lon),
        rdma(pack_low, corner.at[3], 6, 7, lat - 1, east),
        rdma(pack_low, corner.at[2], 7, 6, lat - 1, west),
    ]

    to_east.start()
    to_west.start()

    @pl.when(top)
    def _():
        mirror.start()

        @pl.when(fold_e != lon)
        def _():
            mirror_e.start()

        @pl.when(fold_w != lon)
        def _():
            mirror_w.start()

        @pl.when(fold_e == lon)
        def _():
            corner[2] = pack[pl.ds(rows - 8, 8), :]

        @pl.when(fold_w == lon)
        def _():
            corner[3] = pack[pl.ds(rows - 8, 8), :]

    @pl.when(jnp.logical_not(top))
    def _():
        for c in north:
            c.start()

    @pl.when(jnp.logical_not(low))
    def _():
        for c in south:
            c.start()

    nclass = table.shape[1]

    def slopes(idx):
        res = []
        for d in range(2):
            vals = [table[d, k] for k in range(nclass)]
            bit = 1
            while len(vals) > 1:
                on = (idx & bit) != 0
                vals = [jnp.where(on, vals[j + 1], vals[j]) if j + 1 < len(vals) else vals[j]
                        for j in range(0, len(vals), 2)]
                bit *= 2
            res.append(vals[0])
        return res

    def put_slopes(t, r, idx):
        a, b = slopes(idx)
        slope[0, t, pl.ds(r, 8), :] = a
        slope[1, t, pl.ds(r, 8), :] = b

    chunks = (rows + 2 * HALO) // 8

    def own_slopes(e):
        r = row_of(PAD + e * 8)
        for t in range(own):
            put_slopes(t, r, ints[1, t, pl.ds(row_of(r - BASE), 8), :])

    part = lane & (HALF - 1)
    lower = lane < HALF

    def own_strips(e):
        r = row_of(PAD + e * 8)

        def context(f, o):
            ref = field_at(f)
            a = pltpu.roll(ref[0, pl.ds(r, 8), :], HALO + o, 1)
            b = pltpu.roll(ref[own - 1, pl.ds(r, 8), :], (5 * HALO + o) % LANES, 1)
            return jnp.where(part < 3 * HALO, a, b)

        q[0, 2, 0, pl.ds(r, 8), :] = jnp.where(lower, context(0, 0), context(1, HALF))
        for f in range(2, FIELDS):
            a = context(f, 0)
            stat[f - 2, edge, pl.ds(r, 8), :] = jnp.where(lower, a, pltpu.roll(a, HALF, 1))

    beyond = (part < HALO) | (part >= 5 * HALO)

    def whole_strips(e):
        r = row_of(PAD + e * 8)
        both = comb[pl.ds(row_of(r - PAD), 8), :]

        def halo(f, o):
            a = pltpu.roll(both, (o + HALF - HALO * f) % LANES, 1)
            b = pltpu.roll(both, (o + 5 * HALO - HALO * f) % LANES, 1)
            return jnp.where(part < HALO, a, b)

        z = jnp.where(lower, halo(0, 0), halo(1, HALF))
        q[0, 2, 0, pl.ds(r, 8), :] = jnp.where(beyond, z, q[0, 2, 0, pl.ds(r, 8), :])
        for f in range(2, FIELDS):
            a = halo(f, 0)
            z = jnp.where(lower, a, pltpu.roll(a, HALF, 1))
            z = jnp.where(beyond, z, stat[f - 2, edge, pl.ds(r, 8), :])
            if f < FIELDS - 1:
                stat[f - 2, edge, pl.ds(r, 8), :] = z
            else:
                put_slopes(edge, r, z.astype(jnp.int32))

    def shifted(x, by):
        r = [pltpu.roll(a, (-by) % LANES, 1) for a in x]
        n = len(x)
        if n == 1:
            return r
        if by > 0:
            return [jnp.where(lane >= LANES - by, r[(t + 1) % n], r[t]) for t in range(n)]
        return [jnp.where(lane < -by, r[t - 1], r[t]) for t in range(n)]

    def coefs(tiles, e):
        r = row_of(PAD + e * 8)

        def rows_at(ref, f, at):
            return [ref[f, t, pl.ds(at, 8), :] for t in tiles]

        u0, v0, m0 = [rows_at(stat, f, r) for f in range(3)]
        v1, m1 = [rows_at(stat, f, r + 1) for f in (1, 2)]
        x0, y0 = [rows_at(slope, f, r) for f in range(2)]
        x1, y1 = [rows_at(slope, f, r + 1) for f in range(2)]
        me, ue, xe, ye = [shifted(x, 1) for x in (m0, u0, x0, y0)]
        for j, t in enumerate(tiles):
            for d, (ma, mb, wa, wb, aa, ab, ba, bb) in enumerate((
                    (m0, me, u0, ue, x0, xe, y0, ye),
                    (m0, m1, v0, v1, y0, y1, x0, x1))):
                m = ma[j] * mb[j]
                vel = 0.5 * (wa[j] + wb[j])
                sa = 0.5 * (aa[j] + ab[j])
                sb = 0.5 * (ba[j] + bb[j])
                speed = jnp.abs(vel)
                coef[4 * d, t, pl.ds(r, 8), :] = m * (0.1 * (1.0 + sa * sa) - jnp.minimum(vel, 0.0))
                coef[4 * d + 1, t, pl.ds(r, 8), :] = m * (0.025 * (sa * sb))
                coef[4 * d + 2, t, pl.ds(r, 8), :] = m * vel
                coef[4 * d + 3, t, pl.ds(r, 8), :] = m * (0.5 * speed * (1.0 - speed))

    def limited(dn, du):
        return jnp.maximum(jnp.minimum(dn, du), jnp.minimum(jnp.maximum(dn, du), 0.0))

    def coef_tiles(f):
        return range(own) if f < 2 else (edge,)

    def q_rows(step, f, r):
        return [[q[step, f, t, pl.ds(r + j, 8), :] for t in range(own if f < 2 else 1)]
                for j in (-1, 0, 1, 2)]

    def lat_flux(step, f, r, k, around):
        qm, q0, q1, q2 = around
        pair = [a + b for a, b in zip(q0, q1)]
        pe, pw = shifted(pair, 1), shifted(pair, -1)
        res = []
        for t in range(len(q0)):
            dn = q1[t] - q0[t]
            lim = limited(dn, jnp.where(k[2][t] > 0, q0[t] - qm[t], q2[t] - q1[t]))
            g = k[0][t] * dn + k[1][t] * (pe[t] - pw[t]) - (k[2][t] * q0[t] + k[3][t] * lim)
            gy[step, f, t, pl.ds(r, 8), :] = g
            res.append(g)
        return res

    def lat_only(step, e):
        r = row_of(PAD + e * 8)
        k = [[coef[j, t, pl.ds(r, 8), :] for t in range(own)] for j in range(4, 8)]
        for f in range(2):
            lat_flux(step, f, r, k, q_rows(step, f, r))

    def stepped(step, f, r, k, masked):
        around = q_rows(step, f, r)
        qm, q0, q1, q2 = around
        qe, qw, qf = shifted(q0, 1), shifted(q0, -1), shifted(q0, 2)
        vert = [a - b for a, b in zip(q1, qm)]
        ve = shifted(vert, 1)
        gx = []
        for t in range(len(q0)):
            dn = qe[t] - q0[t]
            lim = limited(dn, jnp.where(k[2][t] > 0, q0[t] - qw[t], qf[t] - qe[t]))
            gx.append(k[0][t] * dn + k[1][t] * (vert[t] + ve[t]) - (k[2][t] * q0[t] + k[3][t] * lim))
        gw = shifted(gx, -1)
        g = lat_flux(step, f, r, k[4:], around)
        new = []
        for t in range(len(q0)):
            centre = q0[t] * masked[t] if masked is not None else q0[t]
            new.append(centre + (gx[t] - gw[t]) + g[t])
        return new

    def advance(step, fields, group):
        found = []
        for e in group:
            r = row_of(PAD + e * 8)
            tiles = coef_tiles(fields[0])
            k = [[coef[j, t, pl.ds(r, 8), :] for t in tiles] for j in range(8)]
            masked = [stat[2, t, pl.ds(r, 8), :] for t in tiles] if step == 0 else None
            for f in fields:
                found.append((f, r, stepped(step, f, r, k, masked)))
        for f, r, new in found:
            for t in range(len(new)):
                value = new[t] - gy[step, f, t, pl.ds(r - 1, 8), :]
                if step == STEPS - 1 and f < 2:
                    (t_out, s_out)[f][pl.ds(row_of(r - BASE), 8), pl.ds(LANES * t, LANES)] = value
                else:
                    q[step + 1, f, t, pl.ds(r, 8), :] = value

    over_chunks(1, rows // 8, GROUP, each(own_slopes))
    over_chunks(1, rows // 8, GROUP, each(own_strips))
    over_chunks(1, rows // 8 - 1, GROUP, each(functools.partial(coefs, range(own))))
    for step in range(STEPS):
        first = step + 2
        lat_only(step, first - 1)
        over_chunks(first, chunks - 2 * first, GROUP, functools.partial(advance, step, (0, 1)))

    to_east.wait_recv()
    to_west.wait_recv()
    for h in range(rows // LANES):
        comb[pl.ds(HALO + LANES * h, LANES), :] = col_t[:, pl.ds(LANES * h, LANES)].T

    @pl.when(low)
    def _():
        comb[pl.ds(0, 8), :] = jnp.zeros((8, LANES), jnp.float32)
        for f in range(FIELDS):
            for t in range(own):
                field_at(f)[t, pl.ds(PAD, 8), :] = jnp.zeros((8, LANES), jnp.float32)

    @pl.when(jnp.logical_not(low))
    def _():
        north[0].wait_recv()
        north[1].wait_recv()
        north[2].wait_recv()
        comb[pl.ds(0, 8), :] = jnp.where(lane < HALF, corner[0], corner[1])
        for f in range(FIELDS):
            for t in range(own):
                field_at(f)[t, pl.ds(PAD, 8), :] = sbuf[pl.ds(8 * f, 8), pl.ds(LANES * t, LANES)]

    mirror.wait_recv()

    @pl.when(jnp.logical_not(top))
    def _():
        mirror_e.wait_recv()
        mirror_w.wait_recv()
        comb[pl.ds(HALO + rows, 8), :] = jnp.where(lane < HALF, corner[2], corner[3])
        for f in range(FIELDS):
            for t in range(own):
                field_at(f)[t, pl.ds(BASE + rows, 8), :] = nbuf[pl.ds(8 * f, 8), pl.ds(LANES * t, LANES)]

    @pl.when(top)
    def _():
        @pl.when(fold_e != lon)
        def _():
            mirror_e.wait_recv()

        @pl.when(fold_w != lon)
        def _():
            mirror_w.wait_recv()

        def dot(a, b):
            return jnp.dot(a, b, precision=lax.Precision.HIGHEST, preferred_element_type=jnp.float32)

        def iotas(n):
            return (lax.broadcasted_iota(jnp.int32, (n, n), 0), lax.broadcasted_iota(jnp.int32, (n, n), 1))

        i, j = iotas(cols)
        flip = jnp.where(i + j == cols - 1, 1.0, 0.0)
        i, j = iotas(PACKED)
        turn = jnp.where(j == i + 7 - 2 * (i & 7), 1.0, 0.0)
        turned = dot(turn, dot(nbuf[...], flip))
        for f in range(FIELDS):
            sign = -1.0 if f in (2, 3) else 1.0
            for t in range(own):
                field_at(f)[t, pl.ds(BASE + rows, 8), :] = sign * turned[8 * f:8 * f + 8, LANES * t:LANES * t + LANES]
        i, j = iotas(LANES)
        swap = jnp.where(i == ((j + HALF) & 127) + 7 - 2 * (j & 7), 1.0, 0.0)
        i, j = iotas(8)
        turn8 = jnp.where(i + j == 7, 1.0, 0.0)
        mixed = jnp.where(lane >= HALF, corner[2], corner[3])
        mixed = dot(turn8, dot(mixed, swap))
        flipped = ((lane & 63) >= 2 * HALO) & ((lane & 63) < 4 * HALO)
        comb[pl.ds(HALO + rows, 8), :] = jnp.where(flipped, -mixed, mixed)

    for t in range(own):
        for r in (PAD, BASE + rows):
            put_slopes(t, r, stat[3, t, pl.ds(r, 8), :].astype(jnp.int32))
    own_strips(0)
    own_strips(chunks - 1)
    over_chunks(0, chunks, 8, each(whole_strips))

    for e in (0, chunks - 2, chunks - 1):
        coefs(range(own), e)
    over_chunks(0, chunks, 8, each(functools.partial(coefs, (edge,))))

    for step in range(STEPS):
        last = step == STEPS - 1
        if last:
            lat_only(step, 0)
        ends = list(range(last, step + 2)) + list(range(chunks - step - 2, chunks - last))
        advance(step, (0, 1), ends)
        over_chunks(0, chunks, STRIP_GROUP, functools.partial(advance, step, (2,)))

    def merge(e):
        r = row_of(PAD + e * 8)
        both = q[STEPS, 2, 0, pl.ds(r, 8), :]
        for f, out in enumerate((t_out, s_out)):
            o = row_of(r - BASE)
            a = pltpu.roll(both, (LANES - HALO - HALF * f) % LANES, 1)
            b = pltpu.roll(both, (LANES - 5 * HALO - HALF * f) % LANES, 1)
            left = pl.ds(0, LANES)
            right = pl.ds(LANES * (own - 1), LANES)
            out[pl.ds(o, 8), left] = jnp.where(lane < HALO, a, out[pl.ds(o, 8), left])
            out[pl.ds(o, 8), right] = jnp.where(lane >= LANES - HALO, b, out[pl.ds(o, 8), right])

    over_chunks(1, rows // 8, 8, each(merge))

    to_east.wait_send()
    to_west.wait_send()

    @pl.when(top)
    def _():
        mirror.wait_send()

        @pl.when(fold_e != lon)
        def _():
            mirror_e.wait_send()

        @pl.when(fold_w != lon)
        def _():
            mirror_w.wait_send()

    @pl.when(jnp.logical_not(top))
    def _():
        for c in north:
            c.wait_send()

    @pl.when(jnp.logical_not(low))
    def _():
        for c in south:
            c.wait_send()


def local(nlat, nlon, *args):
    rows, cols = args[0].shape
    own = cols // LANES
    tall = rows + 2 * BASE
    f32 = jnp.float32
    any_ = pl.BlockSpec(memory_space=pltpu.HBM)
    vmem = pl.BlockSpec(memory_space=pltpu.VMEM)
    return pl.pallas_call(
        functools.partial(kernel, nlat, nlon),
        out_shape=(jax.ShapeDtypeStruct((rows, cols), f32),) * 2,
        in_specs=[any_, any_, any_, any_, pl.BlockSpec(memory_space=pltpu.SMEM), any_, any_],
        out_specs=(vmem, vmem),
        scratch_shapes=[
            pltpu.VMEM((STEPS + 1, 3, own, tall, LANES), f32),
            pltpu.VMEM((4, own + 1, tall, LANES), f32),
            pltpu.VMEM((2, own + 1, tall, LANES), f32),
            pltpu.VMEM((2, own, rows, LANES), jnp.int32),
            pltpu.VMEM((8, own + 1, tall, LANES), f32),
            pltpu.VMEM((STEPS, 3, own, tall, LANES), f32),
            pltpu.VMEM((rows, LANES), f32),
            pltpu.VMEM((LANES, rows), f32),
            pltpu.VMEM((PACKED, cols), f32),
            pltpu.VMEM((PACKED, cols), f32),
            pltpu.VMEM((LANES, rows), f32),
            pltpu.VMEM((PACKED, cols), f32),
            pltpu.VMEM((PACKED, cols), f32),
            pltpu.VMEM((4, 8, LANES), f32),
            pltpu.VMEM((rows + 2 * HALO, LANES), f32),
            pltpu.SemaphoreType.DMA((FIELDS * own,)),
            pltpu.SemaphoreType.DMA((8,)),
            pltpu.SemaphoreType.DMA((8,)),
        ],
        compiler_params=pltpu.CompilerParams(
            collective_id=0, has_side_effects=True, vmem_limit_bytes=64 * 1024 * 1024 - 65536),
        name="tracer_steps",
    )(*args[:4], args[4].T, *args[5:])


def solution(mesh):
    names = dict(zip(mesh.axis_names, mesh.devices.shape))
    block = P("lat", "lon")
    return jax.shard_map(
        functools.partial(local, names["lat"], names["lon"]),
        mesh=mesh,
        in_specs=(block, block, block, block, P(), block, block),
        out_specs=(block, block),
        check_vma=False,
    )
```

```python
import functools

import jax
import jax.numpy as jnp
from jax import lax
from jax.experimental import pallas as pl
from jax.experimental.pallas import tpu as pltpu
from jax.sharding import PartitionSpec as P

STEPS = 4
HALO = 2 * STEPS
FIELDS = 6
LANES = 128
PAD = 8
BASE = PAD + HALO
PACKED = FIELDS * HALO
HALF = 64
VMEM_BYTES = 64 * 1024 * 1024
MESH = pl.DeviceIdType.MESH


GROUP = 8
STEP_GROUP = 10
STRIP_GROUP = 17
ENDS = STEPS + 1


def over_chunks(first, count, group, body):
    def some(i, _):
        body([first + i * group + j for j in range(group)])
        return 0

    lax.fori_loop(0, count // group, some, 0)
    if count % group:
        body([first + count - count % group + j for j in range(count % group)])


def each(body):
    def run(group):
        for i in group:
            body(i)

    return run


def row_of(r):
    return r if isinstance(r, int) else pl.multiple_of(r, 8)


def lane_index(rows=8):
    return lax.broadcasted_iota(jnp.int32, (rows, LANES), 1)


def kernel(
    nlat, nlon,
    t_in, s_in, m_in, k_in, table, u_in, v_in,
    t_out, s_out,
    q, stat, slope, ints, coef, gy,
    pack, pack_t, tops, bots,
    col_t, nbuf, sbuf, corner, comb,
    load_sem, send_sem, recv_sem,
):
    rows, cols = t_in.shape
    own = cols // LANES
    edge = own
    lat = lax.axis_index("lat")
    lon = lax.axis_index("lon")
    top = lat == nlat - 1
    low = lat == 0
    east = lax.rem(lon + 1, nlon)
    west = lax.rem(lon + nlon - 1, nlon)
    fold = nlon - 1 - lon
    fold_e = lax.rem(2 * nlon - 2 - lon, nlon)
    fold_w = lax.rem(nlon - lon, nlon)

    def field_at(f):
        return q.at[0, f] if f < 2 else stat.at[f - 2]

    loads = []
    for f, ref in enumerate((t_in, s_in, u_in, v_in)):
        for t in range(own):
            loads.append(pltpu.make_async_copy(
                ref.at[:, pl.ds(LANES * t, LANES)],
                field_at(f).at[t, pl.ds(BASE, rows), :],
                load_sem.at[len(loads)]))
    for f, ref in enumerate((m_in, k_in)):
        for t in range(own):
            loads.append(pltpu.make_async_copy(
                ref.at[:, pl.ds(LANES * t, LANES)],
                ints.at[f, t],
                load_sem.at[len(loads)]))
    for c in loads:
        c.start()

    barrier = pltpu.get_barrier_semaphore()

    def greet(a, o):
        pl.semaphore_signal(barrier, inc=1, device_id=(o, a), device_id_type=MESH)

    greet(lat, east)
    greet(lat, west)

    @pl.when(jnp.logical_not(top))
    def _():
        greet(lat + 1, lon)
        greet(lat + 1, east)
        greet(lat + 1, west)

    @pl.when(jnp.logical_not(low))
    def _():
        greet(lat - 1, lon)
        greet(lat - 1, east)
        greet(lat - 1, west)

    @pl.when(top)
    def _():
        greet(lat, fold)

        @pl.when(fold_e != lon)
        def _():
            greet(lat, fold_e)

        @pl.when(fold_w != lon)
        def _():
            greet(lat, fold_w)

    for c in loads:
        c.wait()

    lane = lane_index()

    def pack_rows(i):
        r = row_of(i * 8)
        out = jnp.zeros((8, LANES), jnp.float32)
        for f in range(FIELDS):
            if f < 4:
                first = field_at(f)[0, pl.ds(BASE + r, 8), :]
                last = field_at(f)[own - 1, pl.ds(BASE + r, 8), :]
            else:
                parts = [ints[f - 4, t, pl.ds(r, 8), :].astype(jnp.float32) for t in range(own)]
                for t in range(own):
                    field_at(f)[t, pl.ds(BASE + r, 8), :] = parts[t]
                first, last = parts[0], parts[-1]
            a = HALO * f
            b = HALF + HALO * f
            out = jnp.where((lane >= a) & (lane < a + HALO),
                            pltpu.roll(first, a, 1) if a else first, out)
            out = jnp.where((lane >= b) & (lane < b + HALO),
                            pltpu.roll(last, (b - (LANES - HALO)) % LANES, 1), out)
        pack[pl.ds(r, 8), :] = out

    over_chunks(0, rows // 8, GROUP, each(pack_rows))
    for h in range(rows // LANES):
        pack_t[:, pl.ds(LANES * h, LANES)] = pack[pl.ds(LANES * h, LANES), :].T
    for f in range(FIELDS):
        for t in range(own):
            tops[pl.ds(8 * f, 8), pl.ds(LANES * t, LANES)] = field_at(f)[t, pl.ds(BASE + rows - 8, 8), :]
            bots[pl.ds(8 * f, 8), pl.ds(LANES * t, LANES)] = field_at(f)[t, pl.ds(BASE, 8), :]

    others = lambda x: jnp.where(x, 1, 0)
    count = 2 + 3 * others(jnp.logical_not(low)) + others(top) * (
        1 + others(fold_e != lon) + others(fold_w != lon)) + 3 * others(jnp.logical_not(top))
    pl.semaphore_wait(barrier, count)

    pack_top = pack.at[pl.ds(rows - 8, 8), :]
    pack_low = pack.at[pl.ds(0, 8), :]
    from_west = col_t.at[pl.ds(HALF, PACKED), :]
    from_east = col_t.at[pl.ds(0, PACKED), :]

    def rdma(src, dst, s, r, a, o):
        return pltpu.make_async_remote_copy(
            src_ref=src, dst_ref=dst, send_sem=send_sem.at[s], recv_sem=recv_sem.at[r],
            device_id=(o, a), device_id_type=MESH)

    to_east = rdma(pack_t.at[pl.ds(HALF, PACKED), :], from_west, 0, 0, lat, east)
    to_west = rdma(pack_t.at[pl.ds(0, PACKED), :], from_east, 1, 1, lat, west)
    north = [
        rdma(tops, sbuf, 2, 3, lat + 1, lon),
        rdma(pack_top, corner.at[1], 3, 5, lat + 1, east),
        rdma(pack_top, corner.at[0], 4, 4, lat + 1, west),
    ]
    mirror = rdma(tops, nbuf, 2, 2, lat, fold)
    mirror_e = rdma(pack_top, corner.at[2], 3, 6, lat, fold_e)
    mirror_w = rdma(pack_top, corner.at[3], 4, 7, lat, fold_w)
    south = [
        rdma(bots, nbuf, 5, 2, lat - 1, lon),
        rdma(pack_low, corner.at[3], 6, 7, lat - 1, east),
        rdma(pack_low, corner.at[2], 7, 6, lat - 1, west),
    ]

    to_east.start()
    to_west.start()

    @pl.when(top)
    def _():
        mirror.start()

        @pl.when(fold_e != lon)
        def _():
            mirror_e.start()

        @pl.when(fold_w != lon)
        def _():
            mirror_w.start()

        @pl.when(fold_e == lon)
        def _():
            corner[2] = pack[pl.ds(rows - 8, 8), :]

        @pl.when(fold_w == lon)
        def _():
            corner[3] = pack[pl.ds(rows - 8, 8), :]

    @pl.when(jnp.logical_not(top))
    def _():
        for c in north:
            c.start()

    @pl.when(jnp.logical_not(low))
    def _():
        for c in south:
            c.start()

    nclass = table.shape[1]

    def slopes(idx):
        res = []
        for d in range(2):
            vals = [table[d, k] for k in range(nclass)]
            bit = 1
            while len(vals) > 1:
                on = (idx & bit) != 0
                vals = [jnp.where(on, vals[j + 1], vals[j]) if j + 1 < len(vals) else vals[j]
                        for j in range(0, len(vals), 2)]
                bit *= 2
            res.append(vals[0])
        return res

    def put_slopes(t, r, idx):
        a, b = slopes(idx)
        slope[0, t, pl.ds(r, 8), :] = a
        slope[1, t, pl.ds(r, 8), :] = b

    chunks = (rows + 2 * HALO) // 8

    def own_slopes(e):
        r = row_of(PAD + e * 8)
        for t in range(own):
            put_slopes(t, r, ints[1, t, pl.ds(row_of(r - BASE), 8), :])

    part = lane & (HALF - 1)
    lower = lane < HALF

    def own_strips(e):
        r = row_of(PAD + e * 8)

        def context(f, o):
            ref = field_at(f)
            a = pltpu.roll(ref[0, pl.ds(r, 8), :], HALO + o, 1)
            b = pltpu.roll(ref[own - 1, pl.ds(r, 8), :], (5 * HALO + o) % LANES, 1)
            return jnp.where(part < 3 * HALO, a, b)

        q[0, 2, 0, pl.ds(r, 8), :] = jnp.where(lower, context(0, 0), context(1, HALF))
        for f in range(2, FIELDS):
            a = context(f, 0)
            stat[f - 2, edge, pl.ds(r, 8), :] = jnp.where(lower, a, pltpu.roll(a, HALF, 1))

    beyond = (part < HALO) | (part >= 5 * HALO)

    def whole_strips(e):
        r = row_of(PAD + e * 8)
        both = comb[pl.ds(row_of(r - PAD), 8), :]

        def halo(f, o):
            a = pltpu.roll(both, (o + HALF - HALO * f) % LANES, 1)
            b = pltpu.roll(both, (o + 5 * HALO - HALO * f) % LANES, 1)
            return jnp.where(part < HALO, a, b)

        z = jnp.where(lower, halo(0, 0), halo(1, HALF))
        q[0, 2, 0, pl.ds(r, 8), :] = jnp.where(beyond, z, q[0, 2, 0, pl.ds(r, 8), :])
        for f in range(2, FIELDS):
            a = halo(f, 0)
            z = jnp.where(lower, a, pltpu.roll(a, HALF, 1))
            z = jnp.where(beyond, z, stat[f - 2, edge, pl.ds(r, 8), :])
            if f < FIELDS - 1:
                stat[f - 2, edge, pl.ds(r, 8), :] = z
            else:
                put_slopes(edge, r, z.astype(jnp.int32))

    def shifted(x, by):
        r = [pltpu.roll(a, (-by) % LANES, 1) for a in x]
        n = len(x)
        if n == 1:
            return r
        if by > 0:
            return [jnp.where(lane >= LANES - by, r[(t + 1) % n], r[t]) for t in range(n)]
        return [jnp.where(lane < -by, r[t - 1], r[t]) for t in range(n)]

    def coefs(tiles, e):
        r = row_of(PAD + e * 8)

        def rows_at(ref, f, at):
            return [ref[f, t, pl.ds(at, 8), :] for t in tiles]

        u0, v0, m0 = [rows_at(stat, f, r) for f in range(3)]
        v1, m1 = [rows_at(stat, f, r + 1) for f in (1, 2)]
        x0, y0 = [rows_at(slope, f, r) for f in range(2)]
        x1, y1 = [rows_at(slope, f, r + 1) for f in range(2)]
        me, ue, xe, ye = [shifted(x, 1) for x in (m0, u0, x0, y0)]
        for j, t in enumerate(tiles):
            for d, (ma, mb, wa, wb, aa, ab, ba, bb) in enumerate((
                    (m0, me, u0, ue, x0, xe, y0, ye),
                    (m0, m1, v0, v1, y0, y1, x0, x1))):
                m = ma[j] * mb[j]
                vel = 0.5 * (wa[j] + wb[j])
                sa = 0.5 * (aa[j] + ab[j])
                sb = 0.5 * (ba[j] + bb[j])
                speed = jnp.abs(vel)
                coef[4 * d, t, pl.ds(r, 8), :] = m * (0.1 * (1.0 + sa * sa) - jnp.minimum(vel, 0.0))
                coef[4 * d + 1, t, pl.ds(r, 8), :] = m * (0.025 * (sa * sb))
                coef[4 * d + 2, t, pl.ds(r, 8), :] = m * vel
                coef[4 * d + 3, t, pl.ds(r, 8), :] = m * (0.5 * speed * (1.0 - speed))

    def limited(dn, du):
        return jnp.maximum(jnp.minimum(dn, du), jnp.minimum(jnp.maximum(dn, du), 0.0))

    def coef_tiles(f):
        return range(own) if f < 2 else (edge,)

    def q_rows(step, f, r):
        return [[q[step, f, t, pl.ds(r + j, 8), :] for t in range(own if f < 2 else 1)]
                for j in (-1, 0, 1, 2)]

    def lat_flux(step, f, r, k, around):
        qm, q0, q1, q2 = around
        pair = [a + b for a, b in zip(q0, q1)]
        pe, pw = shifted(pair, 1), shifted(pair, -1)
        res = []
        for t in range(len(q0)):
            dn = q1[t] - q0[t]
            lim = limited(dn, jnp.where(k[2][t] > 0, q0[t] - qm[t], q2[t] - q1[t]))
            g = k[0][t] * dn + k[1][t] * (pe[t] - pw[t]) - (k[2][t] * q0[t] + k[3][t] * lim)
            gy[step, f, t, pl.ds(r, 8), :] = g
            res.append(g)
        return res

    def lat_only(step, e):
        r = row_of(PAD + e * 8)
        k = [[coef[j, t, pl.ds(r, 8), :] for t in range(own)] for j in range(4, 8)]
        for f in range(2):
            lat_flux(step, f, r, k, q_rows(step, f, r))

    def stepped(step, f, r, k, masked):
        around = q_rows(step, f, r)
        qm, q0, q1, q2 = around
        qe, qw, qf = shifted(q0, 1), shifted(q0, -1), shifted(q0, 2)
        vert = [a - b for a, b in zip(q1, qm)]
        ve = shifted(vert, 1)
        gx = []
        for t in range(len(q0)):
            dn = qe[t] - q0[t]
            lim = limited(dn, jnp.where(k[2][t] > 0, q0[t] - qw[t], qf[t] - qe[t]))
            gx.append(k[0][t] * dn + k[1][t] * (vert[t] + ve[t]) - (k[2][t] * q0[t] + k[3][t] * lim))
        gw = shifted(gx, -1)
        g = lat_flux(step, f, r, k[4:], around)
        new = []
        for t in range(len(q0)):
            new.append(q0[t] * masked[t] + (gx[t] - gw[t]) + g[t])
        return new

    def advance(step, work):
        found = []
        for fields, e in work:
            r = row_of(PAD + e * 8)
            tiles = coef_tiles(fields[0])
            k = [[coef[j, t, pl.ds(r, 8), :] for t in tiles] for j in range(8)]
            masked = [stat[2, t, pl.ds(r, 8), :] for t in tiles]
            for f in fields:
                found.append((f, r, stepped(step, f, r, k, masked)))
        for f, r, new in found:
            for t in range(len(new)):
                q[step + 1, f, t, pl.ds(r, 8), :] = new[t] - gy[step, f, t, pl.ds(r - 1, 8), :]

    over_chunks(1, rows // 8, GROUP, each(own_slopes))
    over_chunks(1, rows // 8, GROUP, each(own_strips))
    over_chunks(1, rows // 8, GROUP, each(functools.partial(coefs, range(own))))

    def interior(step, _):
        lat_only(step, 1)
        over_chunks(2, chunks - 4, STEP_GROUP,
                    lambda group: advance(step, [((0, 1), e) for e in group]))
        return 0

    lax.fori_loop(0, STEPS, interior, 0)

    to_east.wait_recv()
    to_west.wait_recv()
    for h in range(rows // LANES):
        comb[pl.ds(HALO + LANES * h, LANES), :] = col_t[:, pl.ds(LANES * h, LANES)].T

    @pl.when(low)
    def _():
        comb[pl.ds(0, 8), :] = jnp.zeros((8, LANES), jnp.float32)
        for f in range(FIELDS):
            for t in range(own):
                field_at(f)[t, pl.ds(PAD, 8), :] = jnp.zeros((8, LANES), jnp.float32)

    @pl.when(jnp.logical_not(low))
    def _():
        north[0].wait_recv()
        north[1].wait_recv()
        north[2].wait_recv()
        comb[pl.ds(0, 8), :] = jnp.where(lane < HALF, corner[0], corner[1])
        for f in range(FIELDS):
            for t in range(own):
                field_at(f)[t, pl.ds(PAD, 8), :] = sbuf[pl.ds(8 * f, 8), pl.ds(LANES * t, LANES)]

    mirror.wait_recv()

    @pl.when(jnp.logical_not(top))
    def _():
        mirror_e.wait_recv()
        mirror_w.wait_recv()
        comb[pl.ds(HALO + rows, 8), :] = jnp.where(lane < HALF, corner[2], corner[3])
        for f in range(FIELDS):
            for t in range(own):
                field_at(f)[t, pl.ds(BASE + rows, 8), :] = nbuf[pl.ds(8 * f, 8), pl.ds(LANES * t, LANES)]

    @pl.when(top)
    def _():
        @pl.when(fold_e != lon)
        def _():
            mirror_e.wait_recv()

        @pl.when(fold_w != lon)
        def _():
            mirror_w.wait_recv()

        def dot(a, b):
            return jnp.dot(a, b, precision=lax.Precision.HIGHEST, preferred_element_type=jnp.float32)

        def iotas(n):
            return (lax.broadcasted_iota(jnp.int32, (n, n), 0), lax.broadcasted_iota(jnp.int32, (n, n), 1))

        i, j = iotas(cols)
        flip = jnp.where(i + j == cols - 1, 1.0, 0.0)
        i, j = iotas(PACKED)
        turn = jnp.where(j == i + 7 - 2 * (i & 7), 1.0, 0.0)
        turned = dot(turn, dot(nbuf[...], flip))
        for f in range(FIELDS):
            sign = -1.0 if f in (2, 3) else 1.0
            for t in range(own):
                field_at(f)[t, pl.ds(BASE + rows, 8), :] = sign * turned[8 * f:8 * f + 8, LANES * t:LANES * t + LANES]
        i, j = iotas(LANES)
        swap = jnp.where(i == ((j + HALF) & 127) + 7 - 2 * (j & 7), 1.0, 0.0)
        i, j = iotas(8)
        turn8 = jnp.where(i + j == 7, 1.0, 0.0)
        mixed = jnp.where(lane >= HALF, corner[2], corner[3])
        mixed = dot(turn8, dot(mixed, swap))
        flipped = ((lane & 63) >= 2 * HALO) & ((lane & 63) < 4 * HALO)
        comb[pl.ds(HALO + rows, 8), :] = jnp.where(flipped, -mixed, mixed)

    for t in range(own):
        for r in (PAD, BASE + rows):
            put_slopes(t, r, stat[3, t, pl.ds(r, 8), :].astype(jnp.int32))
    own_strips(0)
    own_strips(chunks - 1)
    over_chunks(0, chunks, STRIP_GROUP, each(whole_strips))

    for e in (0, chunks - 2, chunks - 1):
        coefs(range(own), e)
    over_chunks(0, chunks, STRIP_GROUP, each(functools.partial(coefs, (edge,))))

    def rest(step, _):
        ends = list(range(ENDS)) + list(range(chunks - ENDS, chunks))
        advance(step, [((0, 1), e) for e in ends])
        over_chunks(0, chunks, STRIP_GROUP,
                    lambda group: advance(step, [((2,), e) for e in group]))
        return 0

    lax.fori_loop(0, STEPS, rest, 0)

    def merge(e):
        r = row_of(PAD + e * 8)
        both = q[STEPS, 2, 0, pl.ds(r, 8), :]
        for f, out in enumerate((t_out, s_out)):
            o = row_of(r - BASE)
            tiles = [q[STEPS, f, t, pl.ds(r, 8), :] for t in range(own)]
            a = pltpu.roll(both, (LANES - HALO - HALF * f) % LANES, 1)
            b = pltpu.roll(both, (LANES - 5 * HALO - HALF * f) % LANES, 1)
            tiles[0] = jnp.where(lane < HALO, a, tiles[0])
            tiles[-1] = jnp.where(lane >= LANES - HALO, b, tiles[-1])
            for t in range(own):
                out[pl.ds(o, 8), pl.ds(LANES * t, LANES)] = tiles[t]

    over_chunks(1, rows // 8, GROUP, each(merge))

    to_east.wait_send()
    to_west.wait_send()

    @pl.when(top)
    def _():
        mirror.wait_send()

        @pl.when(fold_e != lon)
        def _():
            mirror_e.wait_send()

        @pl.when(fold_w != lon)
        def _():
            mirror_w.wait_send()

    @pl.when(jnp.logical_not(top))
    def _():
        for c in north:
            c.wait_send()

    @pl.when(jnp.logical_not(low))
    def _():
        for c in south:
            c.wait_send()


def write_out(t_in, s_in, t_out, s_out, sem):
    copies = [pltpu.make_async_copy(t_in, t_out, sem.at[0]),
              pltpu.make_async_copy(s_in, s_out, sem.at[1])]
    for c in copies:
        c.start()
    for c in copies:
        c.wait()


def local(nlat, nlon, *args):
    rows, cols = args[0].shape
    own = cols // LANES
    tall = rows + 2 * BASE
    f32 = jnp.float32
    any_ = pl.BlockSpec(memory_space=pltpu.HBM)
    vmem = pl.BlockSpec(memory_space=pltpu.VMEM)
    found = pl.pallas_call(
        functools.partial(kernel, nlat, nlon),
        out_shape=(pltpu.VMEM((rows, cols), f32),) * 2,
        in_specs=[any_, any_, any_, any_, pl.BlockSpec(memory_space=pltpu.SMEM), any_, any_],
        out_specs=(vmem, vmem),
        scratch_shapes=[
            pltpu.VMEM((STEPS + 1, 3, own, tall, LANES), f32),
            pltpu.VMEM((4, own + 1, tall, LANES), f32),
            pltpu.VMEM((2, own + 1, tall, LANES), f32),
            pltpu.VMEM((2, own, rows, LANES), jnp.int32),
            pltpu.VMEM((8, own + 1, tall, LANES), f32),
            pltpu.VMEM((STEPS, 3, own, tall, LANES), f32),
            pltpu.VMEM((rows, LANES), f32),
            pltpu.VMEM((LANES, rows), f32),
            pltpu.VMEM((PACKED, cols), f32),
            pltpu.VMEM((PACKED, cols), f32),
            pltpu.VMEM((LANES, rows), f32),
            pltpu.VMEM((PACKED, cols), f32),
            pltpu.VMEM((PACKED, cols), f32),
            pltpu.VMEM((4, 8, LANES), f32),
            pltpu.VMEM((rows + 2 * HALO, LANES), f32),
            pltpu.SemaphoreType.DMA((FIELDS * own,)),
            pltpu.SemaphoreType.DMA((8,)),
            pltpu.SemaphoreType.DMA((8,)),
        ],
        compiler_params=pltpu.CompilerParams(
            collective_id=0, has_side_effects=True, vmem_limit_bytes=VMEM_BYTES - 2 * rows * cols * 4 - 65536),
        name="tracer_steps",
    )(*args[:4], args[4].T, *args[5:])
    return pl.pallas_call(
        write_out,
        out_shape=(jax.ShapeDtypeStruct((rows, cols), f32),) * 2,
        in_specs=[pl.BlockSpec(memory_space=pl.ANY)] * 2,
        out_specs=(pl.BlockSpec(memory_space=pl.ANY),) * 2,
        scratch_shapes=[pltpu.SemaphoreType.DMA((2,))],
        name="write_out",
    )(*found)


def solution(mesh):
    names = dict(zip(mesh.axis_names, mesh.devices.shape))
    block = P("lat", "lon")
    return jax.shard_map(
        functools.partial(local, names["lat"], names["lon"]),
        mesh=mesh,
        in_specs=(block, block, block, block, P(), block, block),
        out_specs=(block, block),
        check_vma=False,
    )
```

```python
import functools

import jax
import jax.numpy as jnp
from jax import lax
from jax.experimental import pallas as pl
from jax.experimental.pallas import tpu as pltpu
from jax.sharding import PartitionSpec as P

STEPS = 4
HALO = 2 * STEPS
FIELDS = 6
LANES = 128
PAD = 8
BASE = PAD + HALO
PACKED = FIELDS * HALO
HALF = 64
VMEM_BYTES = 64 * 1024 * 1024
MESH = pl.DeviceIdType.MESH


GROUP = 4
STRIP_GROUP = 17


def over_chunks(first, count, group, body):
    def some(i, _):
        body([first + i * group + j for j in range(group)])
        return 0

    lax.fori_loop(0, count // group, some, 0)
    if count % group:
        body([first + count - count % group + j for j in range(count % group)])


def each(body):
    def run(group):
        for i in group:
            body(i)

    return run


def row_of(r):
    return r if isinstance(r, int) else pl.multiple_of(r, 8)


def lane_index(rows=8):
    return lax.broadcasted_iota(jnp.int32, (rows, LANES), 1)


def kernel(
    nlat, nlon,
    t_in, s_in, m_in, k_in, table, u_in, v_in,
    t_out, s_out,
    q, stat, slope, ints, coef, gy,
    pack, pack_t, tops, bots,
    col_t, nbuf, sbuf, corner, comb,
    load_sem, send_sem, recv_sem,
):
    rows, cols = t_in.shape
    own = cols // LANES
    edge = own
    lat = lax.axis_index("lat")
    lon = lax.axis_index("lon")
    top = lat == nlat - 1
    low = lat == 0
    east = lax.rem(lon + 1, nlon)
    west = lax.rem(lon + nlon - 1, nlon)
    fold = nlon - 1 - lon
    fold_e = lax.rem(2 * nlon - 2 - lon, nlon)
    fold_w = lax.rem(nlon - lon, nlon)

    def field_at(f):
        return q.at[0, f] if f < 2 else stat.at[f - 2]

    loads = []
    for f, ref in enumerate((t_in, s_in, u_in, v_in)):
        for t in range(own):
            loads.append(pltpu.make_async_copy(
                ref.at[:, pl.ds(LANES * t, LANES)],
                field_at(f).at[t, pl.ds(BASE, rows), :],
                load_sem.at[len(loads)]))
    for f, ref in enumerate((m_in, k_in)):
        for t in range(own):
            loads.append(pltpu.make_async_copy(
                ref.at[:, pl.ds(LANES * t, LANES)],
                ints.at[f, t],
                load_sem.at[len(loads)]))
    for c in loads:
        c.start()

    barrier = pltpu.get_barrier_semaphore()

    def greet(a, o):
        pl.semaphore_signal(barrier, inc=1, device_id=(o, a), device_id_type=MESH)

    greet(lat, east)
    greet(lat, west)

    @pl.when(jnp.logical_not(top))
    def _():
        greet(lat + 1, lon)
        greet(lat + 1, east)
        greet(lat + 1, west)

    @pl.when(jnp.logical_not(low))
    def _():
        greet(lat - 1, lon)
        greet(lat - 1, east)
        greet(lat - 1, west)

    @pl.when(top)
    def _():
        greet(lat, fold)

        @pl.when(fold_e != lon)
        def _():
            greet(lat, fold_e)

        @pl.when(fold_w != lon)
        def _():
            greet(lat, fold_w)

    for c in loads:
        c.wait()

    lane = lane_index()

    def pack_rows(i):
        r = row_of(i * 8)
        out = jnp.zeros((8, LANES), jnp.float32)
        for f in range(FIELDS):
            if f < 4:
                first = field_at(f)[0, pl.ds(BASE + r, 8), :]
                last = field_at(f)[own - 1, pl.ds(BASE + r, 8), :]
            else:
                parts = [ints[f - 4, t, pl.ds(r, 8), :].astype(jnp.float32) for t in range(own)]
                for t in range(own):
                    field_at(f)[t, pl.ds(BASE + r, 8), :] = parts[t]
                first, last = parts[0], parts[-1]
            a = HALO * f
            b = HALF + HALO * f
            out = jnp.where((lane >= a) & (lane < a + HALO),
                            pltpu.roll(first, a, 1) if a else first, out)
            out = jnp.where((lane >= b) & (lane < b + HALO),
                            pltpu.roll(last, (b - (LANES - HALO)) % LANES, 1), out)
        pack[pl.ds(r, 8), :] = out

    over_chunks(0, rows // 8, GROUP, each(pack_rows))
    for h in range(rows // LANES):
        pack_t[:, pl.ds(LANES * h, LANES)] = pack[pl.ds(LANES * h, LANES), :].T
    for f in range(FIELDS):
        for t in range(own):
            tops[pl.ds(8 * f, 8), pl.ds(LANES * t, LANES)] = field_at(f)[t, pl.ds(BASE + rows - 8, 8), :]
            bots[pl.ds(8 * f, 8), pl.ds(LANES * t, LANES)] = field_at(f)[t, pl.ds(BASE, 8), :]

    nclass = table.shape[1]

    def slopes(idx):
        res = []
        for d in range(2):
            vals = [table[d, k] for k in range(nclass)]
            bit = 1
            while len(vals) > 1:
                on = (idx & bit) != 0
                vals = [jnp.where(on, vals[j + 1], vals[j]) if j + 1 < len(vals) else vals[j]
                        for j in range(0, len(vals), 2)]
                bit *= 2
            res.append(vals[0])
        return res

    def put_slopes(t, r, idx):
        a, b = slopes(idx)
        slope[0, t, pl.ds(r, 8), :] = a
        slope[1, t, pl.ds(r, 8), :] = b

    chunks = (rows + 2 * HALO) // 8

    def own_slopes(e):
        r = row_of(PAD + e * 8)
        for t in range(own):
            put_slopes(t, r, ints[1, t, pl.ds(row_of(r - BASE), 8), :])

    part = lane & (HALF - 1)
    lower = lane < HALF

    def own_strips(e):
        r = row_of(PAD + e * 8)

        def context(f, o):
            ref = field_at(f)
            a = pltpu.roll(ref[0, pl.ds(r, 8), :], HALO + o, 1)
            b = pltpu.roll(ref[own - 1, pl.ds(r, 8), :], (5 * HALO + o) % LANES, 1)
            return jnp.where(part < 3 * HALO, a, b)

        q[0, 2, 0, pl.ds(r, 8), :] = jnp.where(lower, context(0, 0), context(1, HALF))
        for f in range(2, FIELDS):
            a = context(f, 0)
            stat[f - 2, edge, pl.ds(r, 8), :] = jnp.where(lower, a, pltpu.roll(a, HALF, 1))

    beyond = (part < HALO) | (part >= 5 * HALO)

    def whole_strips(e):
        r = row_of(PAD + e * 8)
        both = comb[pl.ds(row_of(r - PAD), 8), :]

        def halo(f, o):
            a = pltpu.roll(both, (o + HALF - HALO * f) % LANES, 1)
            b = pltpu.roll(both, (o + 5 * HALO - HALO * f) % LANES, 1)
            return jnp.where(part < HALO, a, b)

        z = jnp.where(lower, halo(0, 0), halo(1, HALF))
        q[0, 2, 0, pl.ds(r, 8), :] = jnp.where(beyond, z, q[0, 2, 0, pl.ds(r, 8), :])
        for f in range(2, FIELDS):
            a = halo(f, 0)
            z = jnp.where(lower, a, pltpu.roll(a, HALF, 1))
            z = jnp.where(beyond, z, stat[f - 2, edge, pl.ds(r, 8), :])
            if f < FIELDS - 1:
                stat[f - 2, edge, pl.ds(r, 8), :] = z
            else:
                put_slopes(edge, r, z.astype(jnp.int32))

    def shifted(x, by):
        r = [pltpu.roll(a, (-by) % LANES, 1) for a in x]
        n = len(x)
        if n == 1:
            return r
        if by > 0:
            return [jnp.where(lane >= LANES - by, r[(t + 1) % n], r[t]) for t in range(n)]
        return [jnp.where(lane < -by, r[t - 1], r[t]) for t in range(n)]

    def coefs(tiles, e):
        r = row_of(PAD + e * 8)

        def rows_at(ref, f, at):
            return [ref[f, t, pl.ds(at, 8), :] for t in tiles]

        u0, v0, m0 = [rows_at(stat, f, r) for f in range(3)]
        v1, m1 = [rows_at(stat, f, r + 1) for f in (1, 2)]
        x0, y0 = [rows_at(slope, f, r) for f in range(2)]
        x1, y1 = [rows_at(slope, f, r + 1) for f in range(2)]
        me, ue, xe, ye = [shifted(x, 1) for x in (m0, u0, x0, y0)]
        for j, t in enumerate(tiles):
            for d, (ma, mb, wa, wb, aa, ab, ba, bb) in enumerate((
                    (m0, me, u0, ue, x0, xe, y0, ye),
                    (m0, m1, v0, v1, y0, y1, x0, x1))):
                m = ma[j] * mb[j]
                vel = 0.5 * (wa[j] + wb[j])
                sa = 0.5 * (aa[j] + ab[j])
                sb = 0.5 * (ba[j] + bb[j])
                speed = jnp.abs(vel)
                coef[4 * d, t, pl.ds(r, 8), :] = m * (0.1 * (1.0 + sa * sa) - jnp.minimum(vel, 0.0))
                coef[4 * d + 1, t, pl.ds(r, 8), :] = m * (0.025 * (sa * sb))
                coef[4 * d + 2, t, pl.ds(r, 8), :] = m * vel
                coef[4 * d + 3, t, pl.ds(r, 8), :] = m * (0.5 * speed * (1.0 - speed))

    def limited(dn, du):
        return jnp.maximum(jnp.minimum(dn, du), jnp.minimum(jnp.maximum(dn, du), 0.0))

    def coef_tiles(f):
        return range(own) if f < 2 else (edge,)

    def q_rows(step, f, r):
        return [[q[step, f, t, pl.ds(r + j, 8), :] for t in range(own if f < 2 else 1)]
                for j in (-1, 0, 1, 2)]

    def lat_flux(step, f, r, k, around):
        qm, q0, q1, q2 = around
        pair = [a + b for a, b in zip(q0, q1)]
        pe, pw = shifted(pair, 1), shifted(pair, -1)
        res = []
        for t in range(len(q0)):
            dn = q1[t] - q0[t]
            lim = limited(dn, jnp.where(k[2][t] > 0, q0[t] - qm[t], q2[t] - q1[t]))
            g = k[0][t] * dn + k[1][t] * (pe[t] - pw[t]) - (k[2][t] * q0[t] + k[3][t] * lim)
            gy[step, f, t, pl.ds(r, 8), :] = g
            res.append(g)
        return res

    def lat_only(step, e):
        r = row_of(PAD + e * 8)
        k = [[coef[j, t, pl.ds(r, 8), :] for t in range(own)] for j in range(4, 8)]
        for f in range(2):
            lat_flux(step, f, r, k, q_rows(step, f, r))

    def stepped(step, f, r, k, masked):
        around = q_rows(step, f, r)
        qm, q0, q1, q2 = around
        qe, qw, qf = shifted(q0, 1), shifted(q0, -1), shifted(q0, 2)
        vert = [a - b for a, b in zip(q1, qm)]
        ve = shifted(vert, 1)
        gx = []
        for t in range(len(q0)):
            dn = qe[t] - q0[t]
            lim = limited(dn, jnp.where(k[2][t] > 0, q0[t] - qw[t], qf[t] - qe[t]))
            gx.append(k[0][t] * dn + k[1][t] * (vert[t] + ve[t]) - (k[2][t] * q0[t] + k[3][t] * lim))
        gw = shifted(gx, -1)
        g = lat_flux(step, f, r, k[4:], around)
        new = []
        for t in range(len(q0)):
            centre = q0[t] * masked[t] if masked is not None else q0[t]
            new.append(centre + (gx[t] - gw[t]) + g[t])
        return new

    def advance(step, fields, group):
        found = []
        for e in group:
            r = row_of(PAD + e * 8)
            tiles = coef_tiles(fields[0])
            k = [[coef[j, t, pl.ds(r, 8), :] for t in tiles] for j in range(8)]
            masked = [stat[2, t, pl.ds(r, 8), :] for t in tiles] if step == 0 else None
            for f in fields:
                found.append((f, r, stepped(step, f, r, k, masked)))
        for f, r, new in found:
            for t in range(len(new)):
                value = new[t] - gy[step, f, t, pl.ds(r - 1, 8), :]
                if step == STEPS - 1 and f < 2:
                    (t_out, s_out)[f][pl.ds(row_of(r - BASE), 8), pl.ds(LANES * t, LANES)] = value
                else:
                    q[step + 1, f, t, pl.ds(r, 8), :] = value

    over_chunks(1, rows // 8, GROUP, each(own_slopes))
    over_chunks(1, rows // 8, GROUP, each(own_strips))
    over_chunks(1, rows // 8 - 1, GROUP, each(functools.partial(coefs, range(own))))
    others = lambda x: jnp.where(x, 1, 0)
    count = 2 + 3 * others(jnp.logical_not(low)) + others(top) * (
        1 + others(fold_e != lon) + others(fold_w != lon)) + 3 * others(jnp.logical_not(top))
    pl.semaphore_wait(barrier, count)

    pack_top = pack.at[pl.ds(rows - 8, 8), :]
    pack_low = pack.at[pl.ds(0, 8), :]
    from_west = col_t.at[pl.ds(HALF, PACKED), :]
    from_east = col_t.at[pl.ds(0, PACKED), :]

    def rdma(src, dst, s, r, a, o):
        return pltpu.make_async_remote_copy(
            src_ref=src, dst_ref=dst, send_sem=send_sem.at[s], recv_sem=recv_sem.at[r],
            device_id=(o, a), device_id_type=MESH)

    to_east = rdma(pack_t.at[pl.ds(HALF, PACKED), :], from_west, 0, 0, lat, east)
    to_west = rdma(pack_t.at[pl.ds(0, PACKED), :], from_east, 1, 1, lat, west)
    north = [
        rdma(tops, sbuf, 2, 3, lat + 1, lon),
        rdma(pack_top, corner.at[1], 3, 5, lat + 1, east),
        rdma(pack_top, corner.at[0], 4, 4, lat + 1, west),
    ]
    mirror = rdma(tops, nbuf, 2, 2, lat, fold)
    mirror_e = rdma(pack_top, corner.at[2], 3, 6, lat, fold_e)
    mirror_w = rdma(pack_top, corner.at[3], 4, 7, lat, fold_w)
    south = [
        rdma(bots, nbuf, 5, 2, lat - 1, lon),
        rdma(pack_low, corner.at[3], 6, 7, lat - 1, east),
        rdma(pack_low, corner.at[2], 7, 6, lat - 1, west),
    ]

    to_east.start()
    to_west.start()

    @pl.when(top)
    def _():
        mirror.start()

        @pl.when(fold_e != lon)
        def _():
            mirror_e.start()

        @pl.when(fold_w != lon)
        def _():
            mirror_w.start()

        @pl.when(fold_e == lon)
        def _():
            corner[2] = pack[pl.ds(rows - 8, 8), :]

        @pl.when(fold_w == lon)
        def _():
            corner[3] = pack[pl.ds(rows - 8, 8), :]

    @pl.when(jnp.logical_not(top))
    def _():
        for c in north:
            c.start()

    @pl.when(jnp.logical_not(low))
    def _():
        for c in south:
            c.start()

    for step in range(STEPS):
        first = step + 2
        lat_only(step, first - 1)
        over_chunks(first, chunks - 2 * first, GROUP, functools.partial(advance, step, (0, 1)))

    to_east.wait_recv()
    to_west.wait_recv()
    for h in range(rows // LANES):
        comb[pl.ds(HALO + LANES * h, LANES), :] = col_t[:, pl.ds(LANES * h, LANES)].T

    @pl.when(low)
    def _():
        comb[pl.ds(0, 8), :] = jnp.zeros((8, LANES), jnp.float32)
        for f in range(FIELDS):
            for t in range(own):
                field_at(f)[t, pl.ds(PAD, 8), :] = jnp.zeros((8, LANES), jnp.float32)

    @pl.when(jnp.logical_not(low))
    def _():
        north[0].wait_recv()
        north[1].wait_recv()
        north[2].wait_recv()
        comb[pl.ds(0, 8), :] = jnp.where(lane < HALF, corner[0], corner[1])
        for f in range(FIELDS):
            for t in range(own):
                field_at(f)[t, pl.ds(PAD, 8), :] = sbuf[pl.ds(8 * f, 8), pl.ds(LANES * t, LANES)]

    mirror.wait_recv()

    @pl.when(jnp.logical_not(top))
    def _():
        mirror_e.wait_recv()
        mirror_w.wait_recv()
        comb[pl.ds(HALO + rows, 8), :] = jnp.where(lane < HALF, corner[2], corner[3])
        for f in range(FIELDS):
            for t in range(own):
                field_at(f)[t, pl.ds(BASE + rows, 8), :] = nbuf[pl.ds(8 * f, 8), pl.ds(LANES * t, LANES)]

    @pl.when(top)
    def _():
        @pl.when(fold_e != lon)
        def _():
            mirror_e.wait_recv()

        @pl.when(fold_w != lon)
        def _():
            mirror_w.wait_recv()

        def dot(a, b):
            return jnp.dot(a, b, precision=lax.Precision.HIGHEST, preferred_element_type=jnp.float32)

        def iotas(n):
            return (lax.broadcasted_iota(jnp.int32, (n, n), 0), lax.broadcasted_iota(jnp.int32, (n, n), 1))

        i, j = iotas(cols)
        flip = jnp.where(i + j == cols - 1, 1.0, 0.0)
        i, j = iotas(PACKED)
        turn = jnp.where(j == i + 7 - 2 * (i & 7), 1.0, 0.0)
        turned = dot(turn, dot(nbuf[...], flip))
        for f in range(FIELDS):
            sign = -1.0 if f in (2, 3) else 1.0
            for t in range(own):
                field_at(f)[t, pl.ds(BASE + rows, 8), :] = sign * turned[8 * f:8 * f + 8, LANES * t:LANES * t + LANES]
        i, j = iotas(LANES)
        swap = jnp.where(i == ((j + HALF) & 127) + 7 - 2 * (j & 7), 1.0, 0.0)
        i, j = iotas(8)
        turn8 = jnp.where(i + j == 7, 1.0, 0.0)
        mixed = jnp.where(lane >= HALF, corner[2], corner[3])
        mixed = dot(turn8, dot(mixed, swap))
        flipped = ((lane & 63) >= 2 * HALO) & ((lane & 63) < 4 * HALO)
        comb[pl.ds(HALO + rows, 8), :] = jnp.where(flipped, -mixed, mixed)

    for t in range(own):
        for r in (PAD, BASE + rows):
            put_slopes(t, r, stat[3, t, pl.ds(r, 8), :].astype(jnp.int32))
    own_strips(0)
    own_strips(chunks - 1)
    over_chunks(0, chunks, 8, each(whole_strips))

    for e in (0, chunks - 2, chunks - 1):
        coefs(range(own), e)
    over_chunks(0, chunks, 8, each(functools.partial(coefs, (edge,))))

    for step in range(STEPS):
        last = step == STEPS - 1
        if last:
            lat_only(step, 0)
        ends = list(range(last, step + 2)) + list(range(chunks - step - 2, chunks - last))
        for j in range(0, len(ends), GROUP):
            advance(step, (0, 1), ends[j:j + GROUP])
        over_chunks(0, chunks, STRIP_GROUP, functools.partial(advance, step, (2,)))

    def merge(e):
        r = row_of(PAD + e * 8)
        both = q[STEPS, 2, 0, pl.ds(r, 8), :]
        for f, out in enumerate((t_out, s_out)):
            o = row_of(r - BASE)
            a = pltpu.roll(both, (LANES - HALO - HALF * f) % LANES, 1)
            b = pltpu.roll(both, (LANES - 5 * HALO - HALF * f) % LANES, 1)
            left = pl.ds(0, LANES)
            right = pl.ds(LANES * (own - 1), LANES)
            out[pl.ds(o, 8), left] = jnp.where(lane < HALO, a, out[pl.ds(o, 8), left])
            out[pl.ds(o, 8), right] = jnp.where(lane >= LANES - HALO, b, out[pl.ds(o, 8), right])

    over_chunks(1, rows // 8, 8, each(merge))

    to_east.wait_send()
    to_west.wait_send()

    @pl.when(top)
    def _():
        mirror.wait_send()

        @pl.when(fold_e != lon)
        def _():
            mirror_e.wait_send()

        @pl.when(fold_w != lon)
        def _():
            mirror_w.wait_send()

    @pl.when(jnp.logical_not(top))
    def _():
        for c in north:
            c.wait_send()

    @pl.when(jnp.logical_not(low))
    def _():
        for c in south:
            c.wait_send()


def local(nlat, nlon, *args):
    rows, cols = args[0].shape
    own = cols // LANES
    tall = rows + 2 * BASE
    f32 = jnp.float32
    any_ = pl.BlockSpec(memory_space=pltpu.HBM)
    vmem = pl.BlockSpec(memory_space=pltpu.VMEM)
    return pl.pallas_call(
        functools.partial(kernel, nlat, nlon),
        out_shape=(pltpu.VMEM((rows, cols), f32),) * 2,
        in_specs=[any_, any_, any_, any_, pl.BlockSpec(memory_space=pltpu.SMEM), any_, any_],
        out_specs=(vmem, vmem),
        scratch_shapes=[
            pltpu.VMEM((STEPS + 1, 3, own, tall, LANES), f32),
            pltpu.VMEM((4, own + 1, tall, LANES), f32),
            pltpu.VMEM((2, own + 1, tall, LANES), f32),
            pltpu.VMEM((2, own, rows, LANES), jnp.int32),
            pltpu.VMEM((8, own + 1, tall, LANES), f32),
            pltpu.VMEM((STEPS, 3, own, tall, LANES), f32),
            pltpu.VMEM((rows, LANES), f32),
            pltpu.VMEM((LANES, rows), f32),
            pltpu.VMEM((PACKED, cols), f32),
            pltpu.VMEM((PACKED, cols), f32),
            pltpu.VMEM((LANES, rows), f32),
            pltpu.VMEM((PACKED, cols), f32),
            pltpu.VMEM((PACKED, cols), f32),
            pltpu.VMEM((4, 8, LANES), f32),
            pltpu.VMEM((rows + 2 * HALO, LANES), f32),
            pltpu.SemaphoreType.DMA((FIELDS * own,)),
            pltpu.SemaphoreType.DMA((8,)),
            pltpu.SemaphoreType.DMA((8,)),
        ],
        compiler_params=pltpu.CompilerParams(
            collective_id=0, has_side_effects=True, vmem_limit_bytes=VMEM_BYTES - 2 * rows * cols * 4 - 65536),
        name="tracer_steps",
    )(*args[:4], args[4].T, *args[5:])


def solution(mesh):
    names = dict(zip(mesh.axis_names, mesh.devices.shape))
    block = P("lat", "lon")
    return jax.shard_map(
        functools.partial(local, names["lat"], names["lon"]),
        mesh=mesh,
        in_specs=(block, block, block, block, P(), block, block),
        out_specs=(block, block),
        check_vma=False,
    )
```

```python
import functools

import jax
import jax.numpy as jnp
from jax import lax
from jax.experimental import pallas as pl
from jax.experimental.pallas import tpu as pltpu
from jax.sharding import PartitionSpec as P

STEPS = 4
HALO = 2 * STEPS
FIELDS = 6
LANES = 128
PAD = 8
BASE = PAD + HALO
PACKED = FIELDS * HALO
HALF = 64
VMEM_BYTES = 64 * 1024 * 1024
MESH = pl.DeviceIdType.MESH


GROUP = 4
STRIP_GROUP = 17


def over_chunks(first, count, group, body):
    def some(i, _):
        body([first + i * group + j for j in range(group)])
        return 0

    lax.fori_loop(0, count // group, some, 0)
    if count % group:
        body([first + count - count % group + j for j in range(count % group)])


def each(body):
    def run(group):
        for i in group:
            body(i)

    return run


def row_of(r):
    return r if isinstance(r, int) else pl.multiple_of(r, 8)


def lane_index(rows=8):
    return lax.broadcasted_iota(jnp.int32, (rows, LANES), 1)


def kernel(
    nlat, nlon,
    t_in, s_in, m_in, k_in, table, u_in, v_in,
    t_out, s_out,
    q, stat, slope, ints, coef, gy,
    pack, pack_t, tops, bots,
    col_t, nbuf, sbuf, corner, comb,
    load_sem, send_sem, recv_sem,
):
    rows, cols = t_in.shape
    own = cols // LANES
    edge = own
    lat = lax.axis_index("lat")
    lon = lax.axis_index("lon")
    top = lat == nlat - 1
    low = lat == 0
    east = lax.rem(lon + 1, nlon)
    west = lax.rem(lon + nlon - 1, nlon)
    fold = nlon - 1 - lon
    fold_e = lax.rem(2 * nlon - 2 - lon, nlon)
    fold_w = lax.rem(nlon - lon, nlon)

    def field_at(f):
        return q.at[0, f] if f < 2 else stat.at[f - 2]

    loads = []
    for f, ref in enumerate((t_in, s_in, u_in, v_in)):
        for t in range(own):
            loads.append(pltpu.make_async_copy(
                ref.at[:, pl.ds(LANES * t, LANES)],
                field_at(f).at[t, pl.ds(BASE, rows), :],
                load_sem.at[len(loads)]))
    for f, ref in enumerate((m_in, k_in)):
        for t in range(own):
            loads.append(pltpu.make_async_copy(
                ref.at[:, pl.ds(LANES * t, LANES)],
                ints.at[f, t],
                load_sem.at[len(loads)]))
    for c in loads:
        c.start()

    barrier = pltpu.get_barrier_semaphore()

    def greet(a, o):
        pl.semaphore_signal(barrier, inc=1, device_id=(o, a), device_id_type=MESH)

    greet(lat, east)
    greet(lat, west)

    @pl.when(jnp.logical_not(top))
    def _():
        greet(lat + 1, lon)
        greet(lat + 1, east)
        greet(lat + 1, west)

    @pl.when(jnp.logical_not(low))
    def _():
        greet(lat - 1, lon)
        greet(lat - 1, east)
        greet(lat - 1, west)

    @pl.when(top)
    def _():
        greet(lat, fold)

        @pl.when(fold_e != lon)
        def _():
            greet(lat, fold_e)

        @pl.when(fold_w != lon)
        def _():
            greet(lat, fold_w)

    for c in loads:
        c.wait()

    lane = lane_index()

    def pack_rows(i):
        r = row_of(i * 8)
        out = jnp.zeros((8, LANES), jnp.float32)
        for f in range(FIELDS):
            if f < 4:
                first = field_at(f)[0, pl.ds(BASE + r, 8), :]
                last = field_at(f)[own - 1, pl.ds(BASE + r, 8), :]
            else:
                parts = [ints[f - 4, t, pl.ds(r, 8), :].astype(jnp.float32) for t in range(own)]
                for t in range(own):
                    field_at(f)[t, pl.ds(BASE + r, 8), :] = parts[t]
                first, last = parts[0], parts[-1]
            a = HALO * f
            b = HALF + HALO * f
            out = jnp.where((lane >= a) & (lane < a + HALO),
                            pltpu.roll(first, a, 1) if a else first, out)
            out = jnp.where((lane >= b) & (lane < b + HALO),
                            pltpu.roll(last, (b - (LANES - HALO)) % LANES, 1), out)
        pack[pl.ds(r, 8), :] = out

    over_chunks(0, rows // 8, GROUP, each(pack_rows))
    for h in range(rows // LANES):
        pack_t[:, pl.ds(LANES * h, LANES)] = pack[pl.ds(LANES * h, LANES), :].T
    for f in range(FIELDS):
        for t in range(own):
            tops[pl.ds(8 * f, 8), pl.ds(LANES * t, LANES)] = field_at(f)[t, pl.ds(BASE + rows - 8, 8), :]
            bots[pl.ds(8 * f, 8), pl.ds(LANES * t, LANES)] = field_at(f)[t, pl.ds(BASE, 8), :]

    nclass = table.shape[1]

    def slopes(idx):
        res = []
        for d in range(2):
            vals = [table[d, k] for k in range(nclass)]
            bit = 1
            while len(vals) > 1:
                on = (idx & bit) != 0
                vals = [jnp.where(on, vals[j + 1], vals[j]) if j + 1 < len(vals) else vals[j]
                        for j in range(0, len(vals), 2)]
                bit *= 2
            res.append(vals[0])
        return res

    def put_slopes(t, r, idx):
        a, b = slopes(idx)
        slope[0, t, pl.ds(r, 8), :] = a
        slope[1, t, pl.ds(r, 8), :] = b

    chunks = (rows + 2 * HALO) // 8

    def own_slopes(e):
        r = row_of(PAD + e * 8)
        for t in range(own):
            put_slopes(t, r, ints[1, t, pl.ds(row_of(r - BASE), 8), :])

    part = lane & (HALF - 1)
    lower = lane < HALF

    def own_strips(e):
        r = row_of(PAD + e * 8)

        def context(f, o):
            ref = field_at(f)
            a = pltpu.roll(ref[0, pl.ds(r, 8), :], HALO + o, 1)
            b = pltpu.roll(ref[own - 1, pl.ds(r, 8), :], (5 * HALO + o) % LANES, 1)
            return jnp.where(part < 3 * HALO, a, b)

        q[0, 2, 0, pl.ds(r, 8), :] = jnp.where(lower, context(0, 0), context(1, HALF))
        for f in range(2, FIELDS):
            a = context(f, 0)
            stat[f - 2, edge, pl.ds(r, 8), :] = jnp.where(lower, a, pltpu.roll(a, HALF, 1))

    beyond = (part < HALO) | (part >= 5 * HALO)

    def whole_strips(e):
        r = row_of(PAD + e * 8)
        both = comb[pl.ds(row_of(r - PAD), 8), :]

        def halo(f, o):
            a = pltpu.roll(both, (o + HALF - HALO * f) % LANES, 1)
            b = pltpu.roll(both, (o + 5 * HALO - HALO * f) % LANES, 1)
            return jnp.where(part < HALO, a, b)

        z = jnp.where(lower, halo(0, 0), halo(1, HALF))
        q[0, 2, 0, pl.ds(r, 8), :] = jnp.where(beyond, z, q[0, 2, 0, pl.ds(r, 8), :])
        for f in range(2, FIELDS):
            a = halo(f, 0)
            z = jnp.where(lower, a, pltpu.roll(a, HALF, 1))
            z = jnp.where(beyond, z, stat[f - 2, edge, pl.ds(r, 8), :])
            if f < FIELDS - 1:
                stat[f - 2, edge, pl.ds(r, 8), :] = z
            else:
                put_slopes(edge, r, z.astype(jnp.int32))

    def shifted(x, by):
        r = [pltpu.roll(a, (-by) % LANES, 1) for a in x]
        n = len(x)
        if by > 0:
            return [jnp.where(lane >= LANES - by, r[t + 1], r[t]) for t in range(n - 1)] + r[-1:]
        return r[:1] + [jnp.where(lane < -by, r[t - 1], r[t]) for t in range(1, n)]

    def coefs(tiles, e):
        r = row_of(PAD + e * 8)

        def rows_at(ref, f, at):
            return [ref[f, t, pl.ds(at, 8), :] for t in tiles]

        u0, v0, m0 = [rows_at(stat, f, r) for f in range(3)]
        v1, m1 = [rows_at(stat, f, r + 1) for f in (1, 2)]
        x0, y0 = [rows_at(slope, f, r) for f in range(2)]
        x1, y1 = [rows_at(slope, f, r + 1) for f in range(2)]
        me, ue, xe, ye = [shifted(x, 1) for x in (m0, u0, x0, y0)]
        for j, t in enumerate(tiles):
            for d, (ma, mb, wa, wb, aa, ab, ba, bb) in enumerate((
                    (m0, me, u0, ue, x0, xe, y0, ye),
                    (m0, m1, v0, v1, y0, y1, x0, x1))):
                m = ma[j] * mb[j]
                vel = 0.5 * (wa[j] + wb[j])
                sa = 0.5 * (aa[j] + ab[j])
                sb = 0.5 * (ba[j] + bb[j])
                speed = jnp.abs(vel)
                coef[4 * d, t, pl.ds(r, 8), :] = m * (0.1 * (1.0 + sa * sa) - jnp.minimum(vel, 0.0))
                coef[4 * d + 1, t, pl.ds(r, 8), :] = m * (0.025 * (sa * sb))
                coef[4 * d + 2, t, pl.ds(r, 8), :] = m * vel
                coef[4 * d + 3, t, pl.ds(r, 8), :] = m * (0.5 * speed * (1.0 - speed))

    def limited(dn, du):
        return jnp.maximum(jnp.minimum(dn, du), jnp.minimum(jnp.maximum(dn, du), 0.0))

    def coef_tiles(f):
        return range(own) if f < 2 else (edge,)

    def q_rows(step, f, r):
        return [[q[step, f, t, pl.ds(r + j, 8), :] for t in range(own if f < 2 else 1)]
                for j in (-1, 0, 1, 2)]

    def lat_flux(step, f, r, k, around):
        qm, q0, q1, q2 = around
        pair = [a + b for a, b in zip(q0, q1)]
        pe, pw = shifted(pair, 1), shifted(pair, -1)
        for t in range(len(q0)):
            dn = q1[t] - q0[t]
            lim = limited(dn, jnp.where(k[2][t] > 0, q0[t] - qm[t], q2[t] - q1[t]))
            gy[step, f, t, pl.ds(r, 8), :] = (
                k[0][t] * dn + k[1][t] * (pe[t] - pw[t]) - (k[2][t] * q0[t] + k[3][t] * lim))

    def lat_only(step, e):
        r = row_of(PAD + e * 8)
        k = [[coef[j, t, pl.ds(r, 8), :] for t in range(own)] for j in range(4, 8)]
        for f in range(2):
            lat_flux(step, f, r, k, q_rows(step, f, r))

    def lon_and_sum(step, f, r, k, masked):
        tiles = range(own if f < 2 else 1)
        qm, q0, q1 = [[q[step, f, t, pl.ds(r + j, 8), :] for t in tiles] for j in (-1, 0, 1)]
        qe, qw, qf = shifted(q0, 1), shifted(q0, -1), shifted(q0, 2)
        vert = [a - b for a, b in zip(q1, qm)]
        ve = shifted(vert, 1)
        gx = []
        for t in tiles:
            dn = qe[t] - q0[t]
            lim = limited(dn, jnp.where(k[2][t] > 0, q0[t] - qw[t], qf[t] - qe[t]))
            gx.append(k[0][t] * dn + k[1][t] * (vert[t] + ve[t]) - (k[2][t] * q0[t] + k[3][t] * lim))
        gw = shifted(gx, -1)
        for t in tiles:
            centre = q0[t] * masked[t] if masked is not None else q0[t]
            value = (centre + (gx[t] - gw[t])) + (
                gy[step, f, t, pl.ds(r, 8), :] - gy[step, f, t, pl.ds(r - 1, 8), :])
            if step == STEPS - 1 and f < 2:
                (t_out, s_out)[f][pl.ds(row_of(r - BASE), 8), pl.ds(LANES * t, LANES)] = value
            else:
                q[step + 1, f, t, pl.ds(r, 8), :] = value

    def advance(step, fields, group):
        tiles = coef_tiles(fields[0])
        at = [row_of(PAD + e * 8) for e in group]
        for r in at:
            k = [[coef[j, t, pl.ds(r, 8), :] for t in tiles] for j in range(4, 8)]
            for f in fields:
                lat_flux(step, f, r, k, q_rows(step, f, r))
        for r in at:
            k = [[coef[j, t, pl.ds(r, 8), :] for t in tiles] for j in range(4)]
            masked = [stat[2, t, pl.ds(r, 8), :] for t in tiles] if step == 0 else None
            for f in fields:
                lon_and_sum(step, f, r, k, masked)

    over_chunks(1, rows // 8, GROUP, each(own_slopes))
    over_chunks(1, rows // 8, GROUP, each(own_strips))
    over_chunks(1, rows // 8 - 1, GROUP, each(functools.partial(coefs, range(own))))
    def interior(step):
        first = step + 2
        lat_only(step, first - 1)
        over_chunks(first, chunks - 2 * first, GROUP, functools.partial(advance, step, (0, 1)))

    interior(0)

    others = lambda x: jnp.where(x, 1, 0)
    count = 2 + 3 * others(jnp.logical_not(low)) + others(top) * (
        1 + others(fold_e != lon) + others(fold_w != lon)) + 3 * others(jnp.logical_not(top))
    pl.semaphore_wait(barrier, count)

    pack_top = pack.at[pl.ds(rows - 8, 8), :]
    pack_low = pack.at[pl.ds(0, 8), :]
    from_west = col_t.at[pl.ds(HALF, PACKED), :]
    from_east = col_t.at[pl.ds(0, PACKED), :]

    def rdma(src, dst, s, r, a, o):
        return pltpu.make_async_remote_copy(
            src_ref=src, dst_ref=dst, send_sem=send_sem.at[s], recv_sem=recv_sem.at[r],
            device_id=(o, a), device_id_type=MESH)

    to_east = rdma(pack_t.at[pl.ds(HALF, PACKED), :], from_west, 0, 0, lat, east)
    to_west = rdma(pack_t.at[pl.ds(0, PACKED), :], from_east, 1, 1, lat, west)
    north = [
        rdma(tops, sbuf, 2, 3, lat + 1, lon),
        rdma(pack_top, corner.at[1], 3, 5, lat + 1, east),
        rdma(pack_top, corner.at[0], 4, 4, lat + 1, west),
    ]
    mirror = rdma(tops, nbuf, 2, 2, lat, fold)
    mirror_e = rdma(pack_top, corner.at[2], 3, 6, lat, fold_e)
    mirror_w = rdma(pack_top, corner.at[3], 4, 7, lat, fold_w)
    south = [
        rdma(bots, nbuf, 5, 2, lat - 1, lon),
        rdma(pack_low, corner.at[3], 6, 7, lat - 1, east),
        rdma(pack_low, corner.at[2], 7, 6, lat - 1, west),
    ]

    to_east.start()
    to_west.start()

    @pl.when(top)
    def _():
        mirror.start()

        @pl.when(fold_e != lon)
        def _():
            mirror_e.start()

        @pl.when(fold_w != lon)
        def _():
            mirror_w.start()

        @pl.when(fold_e == lon)
        def _():
            corner[2] = pack[pl.ds(rows - 8, 8), :]

        @pl.when(fold_w == lon)
        def _():
            corner[3] = pack[pl.ds(rows - 8, 8), :]

    @pl.when(jnp.logical_not(top))
    def _():
        for c in north:
            c.start()

    @pl.when(jnp.logical_not(low))
    def _():
        for c in south:
            c.start()

    for step in range(1, STEPS):
        interior(step)

    to_east.wait_recv()
    to_west.wait_recv()
    for h in range(rows // LANES):
        comb[pl.ds(HALO + LANES * h, LANES), :] = col_t[:, pl.ds(LANES * h, LANES)].T

    @pl.when(low)
    def _():
        comb[pl.ds(0, 8), :] = jnp.zeros((8, LANES), jnp.float32)
        for f in range(FIELDS):
            for t in range(own):
                field_at(f)[t, pl.ds(PAD, 8), :] = jnp.zeros((8, LANES), jnp.float32)

    @pl.when(jnp.logical_not(low))
    def _():
        north[0].wait_recv()
        north[1].wait_recv()
        north[2].wait_recv()
        comb[pl.ds(0, 8), :] = jnp.where(lane < HALF, corner[0], corner[1])
        for f in range(FIELDS):
            for t in range(own):
                field_at(f)[t, pl.ds(PAD, 8), :] = sbuf[pl.ds(8 * f, 8), pl.ds(LANES * t, LANES)]

    mirror.wait_recv()

    @pl.when(jnp.logical_not(top))
    def _():
        mirror_e.wait_recv()
        mirror_w.wait_recv()
        comb[pl.ds(HALO + rows, 8), :] = jnp.where(lane < HALF, corner[2], corner[3])
        for f in range(FIELDS):
            for t in range(own):
                field_at(f)[t, pl.ds(BASE + rows, 8), :] = nbuf[pl.ds(8 * f, 8), pl.ds(LANES * t, LANES)]

    @pl.when(top)
    def _():
        @pl.when(fold_e != lon)
        def _():
            mirror_e.wait_recv()

        @pl.when(fold_w != lon)
        def _():
            mirror_w.wait_recv()

        def dot(a, b):
            return jnp.dot(a, b, precision=lax.Precision.HIGHEST, preferred_element_type=jnp.float32)

        def iotas(n):
            return (lax.broadcasted_iota(jnp.int32, (n, n), 0), lax.broadcasted_iota(jnp.int32, (n, n), 1))

        i, j = iotas(cols)
        flip = jnp.where(i + j == cols - 1, 1.0, 0.0)
        i, j = iotas(PACKED)
        turn = jnp.where(j == i + 7 - 2 * (i & 7), 1.0, 0.0)
        turned = dot(turn, dot(nbuf[...], flip))
        for f in range(FIELDS):
            sign = -1.0 if f in (2, 3) else 1.0
            for t in range(own):
                field_at(f)[t, pl.ds(BASE + rows, 8), :] = sign * turned[8 * f:8 * f + 8, LANES * t:LANES * t + LANES]
        i, j = iotas(LANES)
        swap = jnp.where(i == ((j + HALF) & 127) + 7 - 2 * (j & 7), 1.0, 0.0)
        i, j = iotas(8)
        turn8 = jnp.where(i + j == 7, 1.0, 0.0)
        mixed = jnp.where(lane >= HALF, corner[2], corner[3])
        mixed = dot(turn8, dot(mixed, swap))
        flipped = ((lane & 63) >= 2 * HALO) & ((lane & 63) < 4 * HALO)
        comb[pl.ds(HALO + rows, 8), :] = jnp.where(flipped, -mixed, mixed)

    for t in range(own):
        for r in (PAD, BASE + rows):
            put_slopes(t, r, stat[3, t, pl.ds(r, 8), :].astype(jnp.int32))
    own_strips(0)
    own_strips(chunks - 1)
    over_chunks(0, chunks, 8, each(whole_strips))

    for e in (0, chunks - 2, chunks - 1):
        coefs(range(own), e)
    over_chunks(0, chunks, 8, each(functools.partial(coefs, (edge,))))

    for step in range(STEPS):
        last = step == STEPS - 1
        if last:
            lat_only(step, 0)
        ends = list(range(last, step + 2)) + list(range(chunks - step - 2, chunks - last))
        for j in range(0, len(ends), GROUP):
            advance(step, (0, 1), ends[j:j + GROUP])
        over_chunks(0, chunks, STRIP_GROUP, functools.partial(advance, step, (2,)))

    def merge(e):
        r = row_of(PAD + e * 8)
        both = q[STEPS, 2, 0, pl.ds(r, 8), :]
        for f, out in enumerate((t_out, s_out)):
            o = row_of(r - BASE)
            a = pltpu.roll(both, (LANES - HALO - HALF * f) % LANES, 1)
            b = pltpu.roll(both, (LANES - 5 * HALO - HALF * f) % LANES, 1)
            left = pl.ds(0, LANES)
            right = pl.ds(LANES * (own - 1), LANES)
            out[pl.ds(o, 8), left] = jnp.where(lane < HALO, a, out[pl.ds(o, 8), left])
            out[pl.ds(o, 8), right] = jnp.where(lane >= LANES - HALO, b, out[pl.ds(o, 8), right])

    over_chunks(1, rows // 8, 8, each(merge))

    to_east.wait_send()
    to_west.wait_send()

    @pl.when(top)
    def _():
        mirror.wait_send()

        @pl.when(fold_e != lon)
        def _():
            mirror_e.wait_send()

        @pl.when(fold_w != lon)
        def _():
            mirror_w.wait_send()

    @pl.when(jnp.logical_not(top))
    def _():
        for c in north:
            c.wait_send()

    @pl.when(jnp.logical_not(low))
    def _():
        for c in south:
            c.wait_send()


def local(nlat, nlon, *args):
    rows, cols = args[0].shape
    own = cols // LANES
    tall = rows + 2 * BASE
    f32 = jnp.float32
    any_ = pl.BlockSpec(memory_space=pltpu.HBM)
    vmem = pl.BlockSpec(memory_space=pltpu.VMEM)
    return pl.pallas_call(
        functools.partial(kernel, nlat, nlon),
        out_shape=(pltpu.VMEM((rows, cols), f32),) * 2,
        in_specs=[any_, any_, any_, any_, pl.BlockSpec(memory_space=pltpu.SMEM), any_, any_],
        out_specs=(vmem, vmem),
        scratch_shapes=[
            pltpu.VMEM((STEPS + 1, 3, own, tall, LANES), f32),
            pltpu.VMEM((4, own + 1, tall, LANES), f32),
            pltpu.VMEM((2, own + 1, tall, LANES), f32),
            pltpu.VMEM((2, own, rows, LANES), jnp.int32),
            pltpu.VMEM((8, own + 1, tall, LANES), f32),
            pltpu.VMEM((STEPS, 3, own, tall, LANES), f32),
            pltpu.VMEM((rows, LANES), f32),
            pltpu.VMEM((LANES, rows), f32),
            pltpu.VMEM((PACKED, cols), f32),
            pltpu.VMEM((PACKED, cols), f32),
            pltpu.VMEM((LANES, rows), f32),
            pltpu.VMEM((PACKED, cols), f32),
            pltpu.VMEM((PACKED, cols), f32),
            pltpu.VMEM((4, 8, LANES), f32),
            pltpu.VMEM((rows + 2 * HALO, LANES), f32),
            pltpu.SemaphoreType.DMA((FIELDS * own,)),
            pltpu.SemaphoreType.DMA((8,)),
            pltpu.SemaphoreType.DMA((8,)),
        ],
        compiler_params=pltpu.CompilerParams(
            collective_id=0, has_side_effects=True, vmem_limit_bytes=VMEM_BYTES - 2 * rows * cols * 4 - 65536),
        name="tracer_steps",
    )(*args[:4], args[4].T, *args[5:])


def solution(mesh):
    names = dict(zip(mesh.axis_names, mesh.devices.shape))
    block = P("lat", "lon")
    return jax.shard_map(
        functools.partial(local, names["lat"], names["lon"]),
        mesh=mesh,
        in_specs=(block, block, block, block, P(), block, block),
        out_specs=(block, block),
        check_vma=False,
    )
```

```python
import functools

import jax
import jax.numpy as jnp
from jax import lax
from jax.experimental import pallas as pl
from jax.experimental.pallas import tpu as pltpu
from jax.sharding import PartitionSpec as P

STEPS = 4
HALO = 2 * STEPS
FIELDS = 6
LANES = 128
PAD = 8
BASE = PAD + HALO
PACKED = FIELDS * HALO
HALF = 64
VMEM_BYTES = 64 * 1024 * 1024
MESH = pl.DeviceIdType.MESH


GROUP = 4
STRIP_GROUP = 17


def over_chunks(first, count, group, body):
    def some(i, _):
        body([first + i * group + j for j in range(group)])
        return 0

    lax.fori_loop(0, count // group, some, 0)
    if count % group:
        body([first + count - count % group + j for j in range(count % group)])


def each(body):
    def run(group):
        for i in group:
            body(i)

    return run


def row_of(r):
    return r if isinstance(r, int) else pl.multiple_of(r, 8)


def lane_index(rows=8):
    return lax.broadcasted_iota(jnp.int32, (rows, LANES), 1)


def kernel(
    nlat, nlon,
    t_in, s_in, m_in, k_in, table, u_in, v_in,
    t_out, s_out,
    q, stat, slope, ints, coef, gy,
    pack, pack_t, tops, bots,
    col_t, nbuf, sbuf, corner, comb,
    load_sem, send_sem, recv_sem,
):
    rows, cols = t_in.shape
    own = cols // LANES
    edge = own
    lat = lax.axis_index("lat")
    lon = lax.axis_index("lon")
    top = lat == nlat - 1
    low = lat == 0
    east = lax.rem(lon + 1, nlon)
    west = lax.rem(lon + nlon - 1, nlon)
    fold = nlon - 1 - lon
    fold_e = lax.rem(2 * nlon - 2 - lon, nlon)
    fold_w = lax.rem(nlon - lon, nlon)

    def field_at(f):
        return q.at[0, f] if f < 2 else stat.at[f - 2]

    loads = []
    for f, ref in enumerate((t_in, s_in, u_in, v_in)):
        for t in range(own):
            loads.append(pltpu.make_async_copy(
                ref.at[:, pl.ds(LANES * t, LANES)],
                field_at(f).at[t, pl.ds(BASE, rows), :],
                load_sem.at[len(loads)]))
    for f, ref in enumerate((m_in, k_in)):
        for t in range(own):
            loads.append(pltpu.make_async_copy(
                ref.at[:, pl.ds(LANES * t, LANES)],
                ints.at[f, t],
                load_sem.at[len(loads)]))
    for c in loads:
        c.start()

    barrier = pltpu.get_barrier_semaphore()

    def greet(a, o):
        pl.semaphore_signal(barrier, inc=1, device_id=(o, a), device_id_type=MESH)

    greet(lat, east)
    greet(lat, west)

    @pl.when(jnp.logical_not(top))
    def _():
        greet(lat + 1, lon)
        greet(lat + 1, east)
        greet(lat + 1, west)

    @pl.when(jnp.logical_not(low))
    def _():
        greet(lat - 1, lon)
        greet(lat - 1, east)
        greet(lat - 1, west)

    @pl.when(top)
    def _():
        greet(lat, fold)

        @pl.when(fold_e != lon)
        def _():
            greet(lat, fold_e)

        @pl.when(fold_w != lon)
        def _():
            greet(lat, fold_w)

    for c in loads:
        c.wait()

    lane = lane_index()

    def pack_rows(i):
        r = row_of(i * 8)
        out = jnp.zeros((8, LANES), jnp.float32)
        for f in range(FIELDS):
            if f < 4:
                first = field_at(f)[0, pl.ds(BASE + r, 8), :]
                last = field_at(f)[own - 1, pl.ds(BASE + r, 8), :]
            else:
                parts = [ints[f - 4, t, pl.ds(r, 8), :].astype(jnp.float32) for t in range(own)]
                for t in range(own):
                    field_at(f)[t, pl.ds(BASE + r, 8), :] = parts[t]
                first, last = parts[0], parts[-1]
            a = HALO * f
            b = HALF + HALO * f
            out = jnp.where((lane >= a) & (lane < a + HALO),
                            pltpu.roll(first, a, 1) if a else first, out)
            out = jnp.where((lane >= b) & (lane < b + HALO),
                            pltpu.roll(last, (b - (LANES - HALO)) % LANES, 1), out)
        pack[pl.ds(r, 8), :] = out

    over_chunks(0, rows // 8, GROUP, each(pack_rows))
    for h in range(rows // LANES):
        pack_t[:, pl.ds(LANES * h, LANES)] = pack[pl.ds(LANES * h, LANES), :].T
    for f in range(FIELDS):
        for t in range(own):
            tops[pl.ds(8 * f, 8), pl.ds(LANES * t, LANES)] = field_at(f)[t, pl.ds(BASE + rows - 8, 8), :]
            bots[pl.ds(8 * f, 8), pl.ds(LANES * t, LANES)] = field_at(f)[t, pl.ds(BASE, 8), :]

    nclass = table.shape[1]

    def slopes(idx):
        res = []
        for d in range(2):
            vals = [table[d, k] for k in range(nclass)]
            bit = 1
            while len(vals) > 1:
                on = (idx & bit) != 0
                vals = [jnp.where(on, vals[j + 1], vals[j]) if j + 1 < len(vals) else vals[j]
                        for j in range(0, len(vals), 2)]
                bit *= 2
            res.append(vals[0])
        return res

    def put_slopes(t, r, idx):
        a, b = slopes(idx)
        slope[0, t, pl.ds(r, 8), :] = a
        slope[1, t, pl.ds(r, 8), :] = b

    chunks = (rows + 2 * HALO) // 8

    def own_slopes(e):
        r = row_of(PAD + e * 8)
        for t in range(own):
            put_slopes(t, r, ints[1, t, pl.ds(row_of(r - BASE), 8), :])

    part = lane & (HALF - 1)
    lower = lane < HALF

    def own_strips(e):
        r = row_of(PAD + e * 8)

        def context(f, o):
            ref = field_at(f)
            a = pltpu.roll(ref[0, pl.ds(r, 8), :], HALO + o, 1)
            b = pltpu.roll(ref[own - 1, pl.ds(r, 8), :], (5 * HALO + o) % LANES, 1)
            return jnp.where(part < 3 * HALO, a, b)

        q[0, 2, 0, pl.ds(r, 8), :] = jnp.where(lower, context(0, 0), context(1, HALF))
        for f in range(2, FIELDS):
            a = context(f, 0)
            stat[f - 2, edge, pl.ds(r, 8), :] = jnp.where(lower, a, pltpu.roll(a, HALF, 1))

    beyond = (part < HALO) | (part >= 5 * HALO)

    def whole_strips(e):
        r = row_of(PAD + e * 8)
        both = comb[pl.ds(row_of(r - PAD), 8), :]

        def halo(f, o):
            a = pltpu.roll(both, (o + HALF - HALO * f) % LANES, 1)
            b = pltpu.roll(both, (o + 5 * HALO - HALO * f) % LANES, 1)
            return jnp.where(part < HALO, a, b)

        z = jnp.where(lower, halo(0, 0), halo(1, HALF))
        q[0, 2, 0, pl.ds(r, 8), :] = jnp.where(beyond, z, q[0, 2, 0, pl.ds(r, 8), :])
        for f in range(2, FIELDS):
            a = halo(f, 0)
            z = jnp.where(lower, a, pltpu.roll(a, HALF, 1))
            z = jnp.where(beyond, z, stat[f - 2, edge, pl.ds(r, 8), :])
            if f < FIELDS - 1:
                stat[f - 2, edge, pl.ds(r, 8), :] = z
            else:
                put_slopes(edge, r, z.astype(jnp.int32))

    def shifted(x, by):
        r = [pltpu.roll(a, (-by) % LANES, 1) for a in x]
        n = len(x)
        if by > 0:
            return [jnp.where(lane >= LANES - by, r[t + 1], r[t]) for t in range(n - 1)] + r[-1:]
        return r[:1] + [jnp.where(lane < -by, r[t - 1], r[t]) for t in range(1, n)]

    def coefs(tiles, e):
        r = row_of(PAD + e * 8)

        def rows_at(ref, f, at):
            return [ref[f, t, pl.ds(at, 8), :] for t in tiles]

        u0, v0, m0 = [rows_at(stat, f, r) for f in range(3)]
        v1, m1 = [rows_at(stat, f, r + 1) for f in (1, 2)]
        x0, y0 = [rows_at(slope, f, r) for f in range(2)]
        x1, y1 = [rows_at(slope, f, r + 1) for f in range(2)]
        me, ue, xe, ye = [shifted(x, 1) for x in (m0, u0, x0, y0)]
        for j, t in enumerate(tiles):
            for d, (ma, mb, wa, wb, aa, ab, ba, bb) in enumerate((
                    (m0, me, u0, ue, x0, xe, y0, ye),
                    (m0, m1, v0, v1, y0, y1, x0, x1))):
                m = ma[j] * mb[j]
                vel = 0.5 * (wa[j] + wb[j])
                sa = 0.5 * (aa[j] + ab[j])
                sb = 0.5 * (ba[j] + bb[j])
                speed = jnp.abs(vel)
                coef[4 * d, t, pl.ds(r, 8), :] = m * (0.1 * (1.0 + sa * sa) - jnp.minimum(vel, 0.0))
                coef[4 * d + 1, t, pl.ds(r, 8), :] = m * (0.025 * (sa * sb))
                coef[4 * d + 2, t, pl.ds(r, 8), :] = m * vel
                coef[4 * d + 3, t, pl.ds(r, 8), :] = m * (0.5 * speed * (1.0 - speed))

    def limited(dn, du):
        return jnp.maximum(jnp.minimum(dn, du), jnp.minimum(jnp.maximum(dn, du), 0.0))

    def coef_tiles(f):
        return range(own) if f < 2 else (edge,)

    def q_rows(step, f, r):
        return [[q[step, f, t, pl.ds(r + j, 8), :] for t in range(own if f < 2 else 1)]
                for j in (-1, 0, 1, 2)]

    def lat_flux(step, f, r, k, around):
        qm, q0, q1, q2 = around
        pair = [a + b for a, b in zip(q0, q1)]
        pe, pw = shifted(pair, 1), shifted(pair, -1)
        res = []
        for t in range(len(q0)):
            dn = q1[t] - q0[t]
            lim = limited(dn, jnp.where(k[2][t] > 0, q0[t] - qm[t], q2[t] - q1[t]))
            g = k[0][t] * dn + k[1][t] * (pe[t] - pw[t]) - (k[2][t] * q0[t] + k[3][t] * lim)
            gy[step, f, t, pl.ds(r, 8), :] = g
            res.append(g)
        return res

    def lat_only(step, e):
        r = row_of(PAD + e * 8)
        k = [[coef[j, t, pl.ds(r, 8), :] for t in range(own)] for j in range(4, 8)]
        for f in range(2):
            lat_flux(step, f, r, k, q_rows(step, f, r))

    def stepped(step, f, r, k, masked):
        around = q_rows(step, f, r)
        qm, q0, q1, q2 = around
        qe, qw, qf = shifted(q0, 1), shifted(q0, -1), shifted(q0, 2)
        vert = [a - b for a, b in zip(q1, qm)]
        ve = shifted(vert, 1)
        gx = []
        for t in range(len(q0)):
            dn = qe[t] - q0[t]
            lim = limited(dn, jnp.where(k[2][t] > 0, q0[t] - qw[t], qf[t] - qe[t]))
            gx.append(k[0][t] * dn + k[1][t] * (vert[t] + ve[t]) - (k[2][t] * q0[t] + k[3][t] * lim))
        gw = shifted(gx, -1)
        g = lat_flux(step, f, r, k[4:], around)
        new = []
        for t in range(len(q0)):
            centre = q0[t] * masked[t] if masked is not None else q0[t]
            new.append(centre + (gx[t] - gw[t]) + g[t])
        return new

    def advance(step, fields, group):
        found = []
        for e in group:
            r = row_of(PAD + e * 8)
            tiles = coef_tiles(fields[0])
            k = [[coef[j, t, pl.ds(r, 8), :] for t in tiles] for j in range(8)]
            masked = [stat[2, t, pl.ds(r, 8), :] for t in tiles] if step == 0 else None
            for f in fields:
                found.append((f, r, stepped(step, f, r, k, masked)))
        for f, r, new in found:
            for t in range(len(new)):
                value = new[t] - gy[step, f, t, pl.ds(r - 1, 8), :]
                if step == STEPS - 1 and f < 2:
                    (t_out, s_out)[f][pl.ds(row_of(r - BASE), 8), pl.ds(LANES * t, LANES)] = value
                else:
                    q[step + 1, f, t, pl.ds(r, 8), :] = value

    over_chunks(1, rows // 8, GROUP, each(own_slopes))
    over_chunks(1, rows // 8, GROUP, each(own_strips))
    others = lambda x: jnp.where(x, 1, 0)
    count = 2 + 3 * others(jnp.logical_not(low)) + others(top) * (
        1 + others(fold_e != lon) + others(fold_w != lon)) + 3 * others(jnp.logical_not(top))
    pl.semaphore_wait(barrier, count)

    pack_top = pack.at[pl.ds(rows - 8, 8), :]
    pack_low = pack.at[pl.ds(0, 8), :]
    from_west = col_t.at[pl.ds(HALF, PACKED), :]
    from_east = col_t.at[pl.ds(0, PACKED), :]

    def rdma(src, dst, s, r, a, o):
        return pltpu.make_async_remote_copy(
            src_ref=src, dst_ref=dst, send_sem=send_sem.at[s], recv_sem=recv_sem.at[r],
            device_id=(o, a), device_id_type=MESH)

    to_east = rdma(pack_t.at[pl.ds(HALF, PACKED), :], from_west, 0, 0, lat, east)
    to_west = rdma(pack_t.at[pl.ds(0, PACKED), :], from_east, 1, 1, lat, west)
    north = [
        rdma(tops, sbuf, 2, 3, lat + 1, lon),
        rdma(pack_top, corner.at[1], 3, 5, lat + 1, east),
        rdma(pack_top, corner.at[0], 4, 4, lat + 1, west),
    ]
    mirror = rdma(tops, nbuf, 2, 2, lat, fold)
    mirror_e = rdma(pack_top, corner.at[2], 3, 6, lat, fold_e)
    mirror_w = rdma(pack_top, corner.at[3], 4, 7, lat, fold_w)
    south = [
        rdma(bots, nbuf, 5, 2, lat - 1, lon),
        rdma(pack_low, corner.at[3], 6, 7, lat - 1, east),
        rdma(pack_low, corner.at[2], 7, 6, lat - 1, west),
    ]

    to_east.start()
    to_west.start()

    @pl.when(top)
    def _():
        mirror.start()

        @pl.when(fold_e != lon)
        def _():
            mirror_e.start()

        @pl.when(fold_w != lon)
        def _():
            mirror_w.start()

        @pl.when(fold_e == lon)
        def _():
            corner[2] = pack[pl.ds(rows - 8, 8), :]

        @pl.when(fold_w == lon)
        def _():
            corner[3] = pack[pl.ds(rows - 8, 8), :]

    @pl.when(jnp.logical_not(top))
    def _():
        for c in north:
            c.start()

    @pl.when(jnp.logical_not(low))
    def _():
        for c in south:
            c.start()

    over_chunks(1, rows // 8 - 1, GROUP, each(functools.partial(coefs, range(own))))
    for step in range(STEPS):
        first = step + 2
        lat_only(step, first - 1)
        over_chunks(first, chunks - 2 * first, GROUP, functools.partial(advance, step, (0, 1)))

    to_east.wait_recv()
    to_west.wait_recv()
    for h in range(rows // LANES):
        comb[pl.ds(HALO + LANES * h, LANES), :] = col_t[:, pl.ds(LANES * h, LANES)].T

    @pl.when(low)
    def _():
        comb[pl.ds(0, 8), :] = jnp.zeros((8, LANES), jnp.float32)
        for f in range(FIELDS):
            for t in range(own):
                field_at(f)[t, pl.ds(PAD, 8), :] = jnp.zeros((8, LANES), jnp.float32)

    @pl.when(jnp.logical_not(low))
    def _():
        north[0].wait_recv()
        north[1].wait_recv()
        north[2].wait_recv()
        comb[pl.ds(0, 8), :] = jnp.where(lane < HALF, corner[0], corner[1])
        for f in range(FIELDS):
            for t in range(own):
                field_at(f)[t, pl.ds(PAD, 8), :] = sbuf[pl.ds(8 * f, 8), pl.ds(LANES * t, LANES)]

    mirror.wait_recv()

    @pl.when(jnp.logical_not(top))
    def _():
        mirror_e.wait_recv()
        mirror_w.wait_recv()
        comb[pl.ds(HALO + rows, 8), :] = jnp.where(lane < HALF, corner[2], corner[3])
        for f in range(FIELDS):
            for t in range(own):
                field_at(f)[t, pl.ds(BASE + rows, 8), :] = nbuf[pl.ds(8 * f, 8), pl.ds(LANES * t, LANES)]

    @pl.when(top)
    def _():
        @pl.when(fold_e != lon)
        def _():
            mirror_e.wait_recv()

        @pl.when(fold_w != lon)
        def _():
            mirror_w.wait_recv()

        def dot(a, b):
            return jnp.dot(a, b, precision=lax.Precision.HIGHEST, preferred_element_type=jnp.float32)

        def iotas(n):
            return (lax.broadcasted_iota(jnp.int32, (n, n), 0), lax.broadcasted_iota(jnp.int32, (n, n), 1))

        i, j = iotas(cols)
        flip = jnp.where(i + j == cols - 1, 1.0, 0.0)
        i, j = iotas(PACKED)
        turn = jnp.where(j == i + 7 - 2 * (i & 7), 1.0, 0.0)
        turned = dot(turn, dot(nbuf[...], flip))
        for f in range(FIELDS):
            sign = -1.0 if f in (2, 3) else 1.0
            for t in range(own):
                field_at(f)[t, pl.ds(BASE + rows, 8), :] = sign * turned[8 * f:8 * f + 8, LANES * t:LANES * t + LANES]
        i, j = iotas(LANES)
        swap = jnp.where(i == ((j + HALF) & 127) + 7 - 2 * (j & 7), 1.0, 0.0)
        i, j = iotas(8)
        turn8 = jnp.where(i + j == 7, 1.0, 0.0)
        mixed = jnp.where(lane >= HALF, corner[2], corner[3])
        mixed = dot(turn8, dot(mixed, swap))
        flipped = ((lane & 63) >= 2 * HALO) & ((lane & 63) < 4 * HALO)
        comb[pl.ds(HALO + rows, 8), :] = jnp.where(flipped, -mixed, mixed)

    for t in range(own):
        for r in (PAD, BASE + rows):
            put_slopes(t, r, stat[3, t, pl.ds(r, 8), :].astype(jnp.int32))
    own_strips(0)
    own_strips(chunks - 1)
    over_chunks(0, chunks, 8, each(whole_strips))

    for e in (0, chunks - 2, chunks - 1):
        coefs(range(own), e)
    over_chunks(0, chunks, 8, each(functools.partial(coefs, (edge,))))

    for step in range(STEPS):
        last = step == STEPS - 1
        if last:
            lat_only(step, 0)
        ends = list(range(last, step + 2)) + list(range(chunks - step - 2, chunks - last))
        for j in range(0, len(ends), GROUP):
            advance(step, (0, 1), ends[j:j + GROUP])
        over_chunks(0, chunks, STRIP_GROUP, functools.partial(advance, step, (2,)))

    def merge(e):
        r = row_of(PAD + e * 8)
        both = q[STEPS, 2, 0, pl.ds(r, 8), :]
        for f, out in enumerate((t_out, s_out)):
            o = row_of(r - BASE)
            a = pltpu.roll(both, (LANES - HALO - HALF * f) % LANES, 1)
            b = pltpu.roll(both, (LANES - 5 * HALO - HALF * f) % LANES, 1)
            left = pl.ds(0, LANES)
            right = pl.ds(LANES * (own - 1), LANES)
            out[pl.ds(o, 8), left] = jnp.where(lane < HALO, a, out[pl.ds(o, 8), left])
            out[pl.ds(o, 8), right] = jnp.where(lane >= LANES - HALO, b, out[pl.ds(o, 8), right])

    over_chunks(1, rows // 8, 8, each(merge))

    to_east.wait_send()
    to_west.wait_send()

    @pl.when(top)
    def _():
        mirror.wait_send()

        @pl.when(fold_e != lon)
        def _():
            mirror_e.wait_send()

        @pl.when(fold_w != lon)
        def _():
            mirror_w.wait_send()

    @pl.when(jnp.logical_not(top))
    def _():
        for c in north:
            c.wait_send()

    @pl.when(jnp.logical_not(low))
    def _():
        for c in south:
            c.wait_send()


def local(nlat, nlon, *args):
    rows, cols = args[0].shape
    own = cols // LANES
    tall = rows + 2 * BASE
    f32 = jnp.float32
    any_ = pl.BlockSpec(memory_space=pltpu.HBM)
    vmem = pl.BlockSpec(memory_space=pltpu.VMEM)
    return pl.pallas_call(
        functools.partial(kernel, nlat, nlon),
        out_shape=(pltpu.VMEM((rows, cols), f32),) * 2,
        in_specs=[any_, any_, any_, any_, pl.BlockSpec(memory_space=pltpu.SMEM), any_, any_],
        out_specs=(vmem, vmem),
        scratch_shapes=[
            pltpu.VMEM((STEPS + 1, 3, own, tall, LANES), f32),
            pltpu.VMEM((4, own + 1, tall, LANES), f32),
            pltpu.VMEM((2, own + 1, tall, LANES), f32),
            pltpu.VMEM((2, own, rows, LANES), jnp.int32),
            pltpu.VMEM((8, own + 1, tall, LANES), f32),
            pltpu.VMEM((STEPS, 3, own, tall, LANES), f32),
            pltpu.VMEM((rows, LANES), f32),
            pltpu.VMEM((LANES, rows), f32),
            pltpu.VMEM((PACKED, cols), f32),
            pltpu.VMEM((PACKED, cols), f32),
            pltpu.VMEM((LANES, rows), f32),
            pltpu.VMEM((PACKED, cols), f32),
            pltpu.VMEM((PACKED, cols), f32),
            pltpu.VMEM((4, 8, LANES), f32),
            pltpu.VMEM((rows + 2 * HALO, LANES), f32),
            pltpu.SemaphoreType.DMA((FIELDS * own,)),
            pltpu.SemaphoreType.DMA((8,)),
            pltpu.SemaphoreType.DMA((8,)),
        ],
        compiler_params=pltpu.CompilerParams(
            collective_id=0, has_side_effects=True, vmem_limit_bytes=VMEM_BYTES - 2 * rows * cols * 4 - 65536),
        name="tracer_steps",
    )(*args[:4], args[4].T, *args[5:])


def solution(mesh):
    names = dict(zip(mesh.axis_names, mesh.devices.shape))
    block = P("lat", "lon")
    return jax.shard_map(
        functools.partial(local, names["lat"], names["lon"]),
        mesh=mesh,
        in_specs=(block, block, block, block, P(), block, block),
        out_specs=(block, block),
        check_vma=False,
    )
```

```python
import functools

import jax
import jax.numpy as jnp
from jax import lax
from jax.experimental import pallas as pl
from jax.experimental.pallas import tpu as pltpu
from jax.sharding import PartitionSpec as P

STEPS = 4
HALO = 2 * STEPS
FIELDS = 6
LANES = 128
PAD = 8
BASE = PAD + HALO
PACKED = FIELDS * HALO
HALF = 64
VMEM_BYTES = 64 * 1024 * 1024
MESH = pl.DeviceIdType.MESH


GROUP = 4
STEP_GROUP = 6
STRIP_GROUP = 17


def over_chunks(first, count, group, body):
    def some(i, _):
        body([first + i * group + j for j in range(group)])
        return 0

    lax.fori_loop(0, count // group, some, 0)
    if count % group:
        body([first + count - count % group + j for j in range(count % group)])


def each(body):
    def run(group):
        for i in group:
            body(i)

    return run


def row_of(r):
    return r if isinstance(r, int) else pl.multiple_of(r, 8)


def lane_index(rows=8):
    return lax.broadcasted_iota(jnp.int32, (rows, LANES), 1)


def kernel(
    nlat, nlon,
    t_in, s_in, m_in, k_in, table, u_in, v_in,
    t_out, s_out,
    q, stat, slope, ints, coef, gy,
    pack, pack_t, tops, bots,
    col_t, nbuf, sbuf, corner, comb,
    load_sem, send_sem, recv_sem,
):
    rows, cols = t_in.shape
    own = cols // LANES
    edge = own
    lat = lax.axis_index("lat")
    lon = lax.axis_index("lon")
    top = lat == nlat - 1
    low = lat == 0
    east = lax.rem(lon + 1, nlon)
    west = lax.rem(lon + nlon - 1, nlon)
    fold = nlon - 1 - lon
    fold_e = lax.rem(2 * nlon - 2 - lon, nlon)
    fold_w = lax.rem(nlon - lon, nlon)

    def field_at(f):
        return q.at[0, f] if f < 2 else stat.at[f - 2]

    loads = []
    for f, ref in enumerate((t_in, s_in, u_in, v_in)):
        for t in range(own):
            loads.append(pltpu.make_async_copy(
                ref.at[:, pl.ds(LANES * t, LANES)],
                field_at(f).at[t, pl.ds(BASE, rows), :],
                load_sem.at[len(loads)]))
    for f, ref in enumerate((m_in, k_in)):
        for t in range(own):
            loads.append(pltpu.make_async_copy(
                ref.at[:, pl.ds(LANES * t, LANES)],
                ints.at[f, t],
                load_sem.at[len(loads)]))
    for c in loads:
        c.start()

    barrier = pltpu.get_barrier_semaphore()

    def greet(a, o):
        pl.semaphore_signal(barrier, inc=1, device_id=(o, a), device_id_type=MESH)

    greet(lat, east)
    greet(lat, west)

    @pl.when(jnp.logical_not(top))
    def _():
        greet(lat + 1, lon)
        greet(lat + 1, east)
        greet(lat + 1, west)

    @pl.when(jnp.logical_not(low))
    def _():
        greet(lat - 1, lon)
        greet(lat - 1, east)
        greet(lat - 1, west)

    @pl.when(top)
    def _():
        greet(lat, fold)

        @pl.when(fold_e != lon)
        def _():
            greet(lat, fold_e)

        @pl.when(fold_w != lon)
        def _():
            greet(lat, fold_w)

    for c in loads:
        c.wait()

    lane = lane_index()

    def pack_rows(i):
        r = row_of(i * 8)
        out = jnp.zeros((8, LANES), jnp.float32)
        for f in range(FIELDS):
            if f < 4:
                first = field_at(f)[0, pl.ds(BASE + r, 8), :]
                last = field_at(f)[own - 1, pl.ds(BASE + r, 8), :]
            else:
                parts = [ints[f - 4, t, pl.ds(r, 8), :].astype(jnp.float32) for t in range(own)]
                for t in range(own):
                    field_at(f)[t, pl.ds(BASE + r, 8), :] = parts[t]
                first, last = parts[0], parts[-1]
            a = HALO * f
            b = HALF + HALO * f
            out = jnp.where((lane >= a) & (lane < a + HALO),
                            pltpu.roll(first, a, 1) if a else first, out)
            out = jnp.where((lane >= b) & (lane < b + HALO),
                            pltpu.roll(last, (b - (LANES - HALO)) % LANES, 1), out)
        pack[pl.ds(r, 8), :] = out

    over_chunks(0, rows // 8, GROUP, each(pack_rows))
    for h in range(rows // LANES):
        pack_t[:, pl.ds(LANES * h, LANES)] = pack[pl.ds(LANES * h, LANES), :].T
    for f in range(FIELDS):
        for t in range(own):
            tops[pl.ds(8 * f, 8), pl.ds(LANES * t, LANES)] = field_at(f)[t, pl.ds(BASE + rows - 8, 8), :]
            bots[pl.ds(8 * f, 8), pl.ds(LANES * t, LANES)] = field_at(f)[t, pl.ds(BASE, 8), :]

    nclass = table.shape[1]

    def slopes(idx):
        res = []
        for d in range(2):
            vals = [table[d, k] for k in range(nclass)]
            bit = 1
            while len(vals) > 1:
                on = (idx & bit) != 0
                vals = [jnp.where(on, vals[j + 1], vals[j]) if j + 1 < len(vals) else vals[j]
                        for j in range(0, len(vals), 2)]
                bit *= 2
            res.append(vals[0])
        return res

    def put_slopes(t, r, idx):
        a, b = slopes(idx)
        slope[0, t, pl.ds(r, 8), :] = a
        slope[1, t, pl.ds(r, 8), :] = b

    chunks = (rows + 2 * HALO) // 8

    def own_slopes(e):
        r = row_of(PAD + e * 8)
        for t in range(own):
            put_slopes(t, r, ints[1, t, pl.ds(row_of(r - BASE), 8), :])

    part = lane & (HALF - 1)
    lower = lane < HALF

    def own_strips(e):
        r = row_of(PAD + e * 8)

        def context(f, o):
            ref = field_at(f)
            a = pltpu.roll(ref[0, pl.ds(r, 8), :], HALO + o, 1)
            b = pltpu.roll(ref[own - 1, pl.ds(r, 8), :], (5 * HALO + o) % LANES, 1)
            return jnp.where(part < 3 * HALO, a, b)

        q[0, 2, 0, pl.ds(r, 8), :] = jnp.where(lower, context(0, 0), context(1, HALF))
        for f in range(2, FIELDS):
            a = context(f, 0)
            stat[f - 2, edge, pl.ds(r, 8), :] = jnp.where(lower, a, pltpu.roll(a, HALF, 1))

    beyond = (part < HALO) | (part >= 5 * HALO)

    def whole_strips(e):
        r = row_of(PAD + e * 8)
        both = comb[pl.ds(row_of(r - PAD), 8), :]

        def halo(f, o):
            a = pltpu.roll(both, (o + HALF - HALO * f) % LANES, 1)
            b = pltpu.roll(both, (o + 5 * HALO - HALO * f) % LANES, 1)
            return jnp.where(part < HALO, a, b)

        z = jnp.where(lower, halo(0, 0), halo(1, HALF))
        q[0, 2, 0, pl.ds(r, 8), :] = jnp.where(beyond, z, q[0, 2, 0, pl.ds(r, 8), :])
        for f in range(2, FIELDS):
            a = halo(f, 0)
            z = jnp.where(lower, a, pltpu.roll(a, HALF, 1))
            z = jnp.where(beyond, z, stat[f - 2, edge, pl.ds(r, 8), :])
            if f < FIELDS - 1:
                stat[f - 2, edge, pl.ds(r, 8), :] = z
            else:
                put_slopes(edge, r, z.astype(jnp.int32))

    def shifted(x, by):
        r = [pltpu.roll(a, (-by) % LANES, 1) for a in x]
        n = len(x)
        if by > 0:
            return [jnp.where(lane >= LANES - by, r[t + 1], r[t]) for t in range(n - 1)] + r[-1:]
        return r[:1] + [jnp.where(lane < -by, r[t - 1], r[t]) for t in range(1, n)]

    def coefs(tiles, e):
        r = row_of(PAD + e * 8)

        def rows_at(ref, f, at):
            return [ref[f, t, pl.ds(at, 8), :] for t in tiles]

        u0, v0, m0 = [rows_at(stat, f, r) for f in range(3)]
        v1, m1 = [rows_at(stat, f, r + 1) for f in (1, 2)]
        x0, y0 = [rows_at(slope, f, r) for f in range(2)]
        x1, y1 = [rows_at(slope, f, r + 1) for f in range(2)]
        me, ue, xe, ye = [shifted(x, 1) for x in (m0, u0, x0, y0)]
        for j, t in enumerate(tiles):
            for d, (ma, mb, wa, wb, aa, ab, ba, bb) in enumerate((
                    (m0, me, u0, ue, x0, xe, y0, ye),
                    (m0, m1, v0, v1, y0, y1, x0, x1))):
                m = ma[j] * mb[j]
                vel = 0.5 * (wa[j] + wb[j])
                sa = 0.5 * (aa[j] + ab[j])
                sb = 0.5 * (ba[j] + bb[j])
                speed = jnp.abs(vel)
                coef[4 * d, t, pl.ds(r, 8), :] = m * (0.1 * (1.0 + sa * sa) - jnp.minimum(vel, 0.0))
                coef[4 * d + 1, t, pl.ds(r, 8), :] = m * (0.025 * (sa * sb))
                coef[4 * d + 2, t, pl.ds(r, 8), :] = m * vel
                coef[4 * d + 3, t, pl.ds(r, 8), :] = m * (0.5 * speed * (1.0 - speed))

    def limited(dn, du):
        return jnp.maximum(jnp.minimum(dn, du), jnp.minimum(jnp.maximum(dn, du), 0.0))

    def coef_tiles(f):
        return range(own) if f < 2 else (edge,)

    def q_rows(step, f, r):
        return [[q[step, f, t, pl.ds(r + j, 8), :] for t in range(own if f < 2 else 1)]
                for j in (-1, 0, 1, 2)]

    def lat_flux(step, f, r, k, around):
        qm, q0, q1, q2 = around
        pair = [a + b for a, b in zip(q0, q1)]
        pe, pw = shifted(pair, 1), shifted(pair, -1)
        res = []
        for t in range(len(q0)):
            dn = q1[t] - q0[t]
            lim = limited(dn, jnp.where(k[2][t] > 0, q0[t] - qm[t], q2[t] - q1[t]))
            g = k[0][t] * dn + k[1][t] * (pe[t] - pw[t]) - (k[2][t] * q0[t] + k[3][t] * lim)
            gy[step, f, t, pl.ds(r, 8), :] = g
            res.append(g)
        return res

    def lat_only(step, e):
        r = row_of(PAD + e * 8)
        k = [[coef[j, t, pl.ds(r, 8), :] for t in range(own)] for j in range(4, 8)]
        for f in range(2):
            lat_flux(step, f, r, k, q_rows(step, f, r))

    def stepped(step, f, r, k, masked):
        around = q_rows(step, f, r)
        qm, q0, q1, q2 = around
        qe, qw, qf = shifted(q0, 1), shifted(q0, -1), shifted(q0, 2)
        vert = [a - b for a, b in zip(q1, qm)]
        ve = shifted(vert, 1)
        gx = []
        for t in range(len(q0)):
            dn = qe[t] - q0[t]
            lim = limited(dn, jnp.where(k[2][t] > 0, q0[t] - qw[t], qf[t] - qe[t]))
            gx.append(k[0][t] * dn + k[1][t] * (vert[t] + ve[t]) - (k[2][t] * q0[t] + k[3][t] * lim))
        gw = shifted(gx, -1)
        g = lat_flux(step, f, r, k[4:], around)
        new = []
        for t in range(len(q0)):
            centre = q0[t] * masked[t] if masked is not None else q0[t]
            new.append(centre + (gx[t] - gw[t]) + g[t])
        return new

    def advance(step, fields, group):
        found = []
        for e in group:
            r = row_of(PAD + e * 8)
            tiles = coef_tiles(fields[0])
            k = [[coef[j, t, pl.ds(r, 8), :] for t in tiles] for j in range(8)]
            masked = [stat[2, t, pl.ds(r, 8), :] for t in tiles] if step == 0 else None
            for f in fields:
                found.append((f, r, stepped(step, f, r, k, masked)))
        for f, r, new in found:
            for t in range(len(new)):
                value = new[t] - gy[step, f, t, pl.ds(r - 1, 8), :]
                if step == STEPS - 1 and f < 2:
                    (t_out, s_out)[f][pl.ds(row_of(r - BASE), 8), pl.ds(LANES * t, LANES)] = value
                else:
                    q[step + 1, f, t, pl.ds(r, 8), :] = value

    over_chunks(1, rows // 8, GROUP, each(own_slopes))
    over_chunks(1, rows // 8, GROUP, each(own_strips))
    others = lambda x: jnp.where(x, 1, 0)
    count = 2 + 3 * others(jnp.logical_not(low)) + others(top) * (
        1 + others(fold_e != lon) + others(fold_w != lon)) + 3 * others(jnp.logical_not(top))
    pl.semaphore_wait(barrier, count)

    pack_top = pack.at[pl.ds(rows - 8, 8), :]
    pack_low = pack.at[pl.ds(0, 8), :]
    from_west = col_t.at[pl.ds(HALF, PACKED), :]
    from_east = col_t.at[pl.ds(0, PACKED), :]

    def rdma(src, dst, s, r, a, o):
        return pltpu.make_async_remote_copy(
            src_ref=src, dst_ref=dst, send_sem=send_sem.at[s], recv_sem=recv_sem.at[r],
            device_id=(o, a), device_id_type=MESH)

    to_east = rdma(pack_t.at[pl.ds(HALF, PACKED), :], from_west, 0, 0, lat, east)
    to_west = rdma(pack_t.at[pl.ds(0, PACKED), :], from_east, 1, 1, lat, west)
    north = [
        rdma(tops, sbuf, 2, 3, lat + 1, lon),
        rdma(pack_top, corner.at[1], 3, 5, lat + 1, east),
        rdma(pack_top, corner.at[0], 4, 4, lat + 1, west),
    ]
    mirror = rdma(tops, nbuf, 2, 2, lat, fold)
    mirror_e = rdma(pack_top, corner.at[2], 3, 6, lat, fold_e)
    mirror_w = rdma(pack_top, corner.at[3], 4, 7, lat, fold_w)
    south = [
        rdma(bots, nbuf, 5, 2, lat - 1, lon),
        rdma(pack_low, corner.at[3], 6, 7, lat - 1, east),
        rdma(pack_low, corner.at[2], 7, 6, lat - 1, west),
    ]

    to_east.start()
    to_west.start()

    @pl.when(top)
    def _():
        mirror.start()

        @pl.when(fold_e != lon)
        def _():
            mirror_e.start()

        @pl.when(fold_w != lon)
        def _():
            mirror_w.start()

        @pl.when(fold_e == lon)
        def _():
            corner[2] = pack[pl.ds(rows - 8, 8), :]

        @pl.when(fold_w == lon)
        def _():
            corner[3] = pack[pl.ds(rows - 8, 8), :]

    @pl.when(jnp.logical_not(top))
    def _():
        for c in north:
            c.start()

    @pl.when(jnp.logical_not(low))
    def _():
        for c in south:
            c.start()

    over_chunks(1, rows // 8 - 1, GROUP, each(functools.partial(coefs, range(own))))
    for step in range(STEPS):
        first = step + 2
        lat_only(step, first - 1)
        over_chunks(first, chunks - 2 * first, STEP_GROUP, functools.partial(advance, step, (0, 1)))

    to_east.wait_recv()
    to_west.wait_recv()
    for h in range(rows // LANES):
        comb[pl.ds(HALO + LANES * h, LANES), :] = col_t[:, pl.ds(LANES * h, LANES)].T

    @pl.when(low)
    def _():
        comb[pl.ds(0, 8), :] = jnp.zeros((8, LANES), jnp.float32)
        for f in range(FIELDS):
            for t in range(own):
                field_at(f)[t, pl.ds(PAD, 8), :] = jnp.zeros((8, LANES), jnp.float32)

    @pl.when(jnp.logical_not(low))
    def _():
        north[0].wait_recv()
        north[1].wait_recv()
        north[2].wait_recv()
        comb[pl.ds(0, 8), :] = jnp.where(lane < HALF, corner[0], corner[1])
        for f in range(FIELDS):
            for t in range(own):
                field_at(f)[t, pl.ds(PAD, 8), :] = sbuf[pl.ds(8 * f, 8), pl.ds(LANES * t, LANES)]

    mirror.wait_recv()

    @pl.when(jnp.logical_not(top))
    def _():
        mirror_e.wait_recv()
        mirror_w.wait_recv()
        comb[pl.ds(HALO + rows, 8), :] = jnp.where(lane < HALF, corner[2], corner[3])
        for f in range(FIELDS):
            for t in range(own):
                field_at(f)[t, pl.ds(BASE + rows, 8), :] = nbuf[pl.ds(8 * f, 8), pl.ds(LANES * t, LANES)]

    @pl.when(top)
    def _():
        @pl.when(fold_e != lon)
        def _():
            mirror_e.wait_recv()

        @pl.when(fold_w != lon)
        def _():
            mirror_w.wait_recv()

        def dot(a, b):
            return jnp.dot(a, b, precision=lax.Precision.HIGHEST, preferred_element_type=jnp.float32)

        def iotas(n):
            return (lax.broadcasted_iota(jnp.int32, (n, n), 0), lax.broadcasted_iota(jnp.int32, (n, n), 1))

        i, j = iotas(cols)
        flip = jnp.where(i + j == cols - 1, 1.0, 0.0)
        i, j = iotas(PACKED)
        turn = jnp.where(j == i + 7 - 2 * (i & 7), 1.0, 0.0)
        turned = dot(turn, dot(nbuf[...], flip))
        for f in range(FIELDS):
            sign = -1.0 if f in (2, 3) else 1.0
            for t in range(own):
                field_at(f)[t, pl.ds(BASE + rows, 8), :] = sign * turned[8 * f:8 * f + 8, LANES * t:LANES * t + LANES]
        i, j = iotas(LANES)
        swap = jnp.where(i == ((j + HALF) & 127) + 7 - 2 * (j & 7), 1.0, 0.0)
        i, j = iotas(8)
        turn8 = jnp.where(i + j == 7, 1.0, 0.0)
        mixed = jnp.where(lane >= HALF, corner[2], corner[3])
        mixed = dot(turn8, dot(mixed, swap))
        flipped = ((lane & 63) >= 2 * HALO) & ((lane & 63) < 4 * HALO)
        comb[pl.ds(HALO + rows, 8), :] = jnp.where(flipped, -mixed, mixed)

    for t in range(own):
        for r in (PAD, BASE + rows):
            put_slopes(t, r, stat[3, t, pl.ds(r, 8), :].astype(jnp.int32))
    own_strips(0)
    own_strips(chunks - 1)
    over_chunks(0, chunks, 8, each(whole_strips))

    for e in (0, chunks - 2, chunks - 1):
        coefs(range(own), e)
    over_chunks(0, chunks, 8, each(functools.partial(coefs, (edge,))))

    for step in range(STEPS):
        last = step == STEPS - 1
        if last:
            lat_only(step, 0)
        ends = list(range(last, step + 2)) + list(range(chunks - step - 2, chunks - last))
        for j in range(0, len(ends), GROUP):
            advance(step, (0, 1), ends[j:j + GROUP])
        over_chunks(0, chunks, STRIP_GROUP, functools.partial(advance, step, (2,)))

    def merge(e):
        r = row_of(PAD + e * 8)
        both = q[STEPS, 2, 0, pl.ds(r, 8), :]
        for f, out in enumerate((t_out, s_out)):
            o = row_of(r - BASE)
            a = pltpu.roll(both, (LANES - HALO - HALF * f) % LANES, 1)
            b = pltpu.roll(both, (LANES - 5 * HALO - HALF * f) % LANES, 1)
            left = pl.ds(0, LANES)
            right = pl.ds(LANES * (own - 1), LANES)
            out[pl.ds(o, 8), left] = jnp.where(lane < HALO, a, out[pl.ds(o, 8), left])
            out[pl.ds(o, 8), right] = jnp.where(lane >= LANES - HALO, b, out[pl.ds(o, 8), right])

    over_chunks(1, rows // 8, 8, each(merge))

    to_east.wait_send()
    to_west.wait_send()

    @pl.when(top)
    def _():
        mirror.wait_send()

        @pl.when(fold_e != lon)
        def _():
            mirror_e.wait_send()

        @pl.when(fold_w != lon)
        def _():
            mirror_w.wait_send()

    @pl.when(jnp.logical_not(top))
    def _():
        for c in north:
            c.wait_send()

    @pl.when(jnp.logical_not(low))
    def _():
        for c in south:
            c.wait_send()


def local(nlat, nlon, *args):
    rows, cols = args[0].shape
    own = cols // LANES
    tall = rows + 2 * BASE
    f32 = jnp.float32
    any_ = pl.BlockSpec(memory_space=pltpu.HBM)
    vmem = pl.BlockSpec(memory_space=pltpu.VMEM)
    return pl.pallas_call(
        functools.partial(kernel, nlat, nlon),
        out_shape=(pltpu.VMEM((rows, cols), f32),) * 2,
        in_specs=[any_, any_, any_, any_, pl.BlockSpec(memory_space=pltpu.SMEM), any_, any_],
        out_specs=(vmem, vmem),
        scratch_shapes=[
            pltpu.VMEM((STEPS + 1, 3, own, tall, LANES), f32),
            pltpu.VMEM((4, own + 1, tall, LANES), f32),
            pltpu.VMEM((2, own + 1, tall, LANES), f32),
            pltpu.VMEM((2, own, rows, LANES), jnp.int32),
            pltpu.VMEM((8, own + 1, tall, LANES), f32),
            pltpu.VMEM((STEPS, 3, own, tall, LANES), f32),
            pltpu.VMEM((rows, LANES), f32),
            pltpu.VMEM((LANES, rows), f32),
            pltpu.VMEM((PACKED, cols), f32),
            pltpu.VMEM((PACKED, cols), f32),
            pltpu.VMEM((LANES, rows), f32),
            pltpu.VMEM((PACKED, cols), f32),
            pltpu.VMEM((PACKED, cols), f32),
            pltpu.VMEM((4, 8, LANES), f32),
            pltpu.VMEM((rows + 2 * HALO, LANES), f32),
            pltpu.SemaphoreType.DMA((FIELDS * own,)),
            pltpu.SemaphoreType.DMA((8,)),
            pltpu.SemaphoreType.DMA((8,)),
        ],
        compiler_params=pltpu.CompilerParams(
            collective_id=0, has_side_effects=True, vmem_limit_bytes=VMEM_BYTES - 2 * rows * cols * 4 - 65536),
        name="tracer_steps",
    )(*args[:4], args[4].T, *args[5:])


def solution(mesh):
    names = dict(zip(mesh.axis_names, mesh.devices.shape))
    block = P("lat", "lon")
    return jax.shard_map(
        functools.partial(local, names["lat"], names["lon"]),
        mesh=mesh,
        in_specs=(block, block, block, block, P(), block, block),
        out_specs=(block, block),
        check_vma=False,
    )
```
